256 devices in a mesh: gx: 4 (over y), gy: 8 (over z), gz: 8 (over x, core).
Axes of the slice: x: 4, y: 4, z: 8, core: 2. Of those that a mesh axis runs over, the one named last changes fastest.
Arguments:
- residual_start: float32 [16, 65536], P(None, ('gx', 'gy', 'gz')), may hold values from -1 to 1
- near_tiles: bfloat16 [32768, 128, 128], P(('gx', 'gy', 'gz')), may hold values from -1 to 1
- near_target: int32 [32768], P(('gx', 'gy', 'gz')), may hold values from 0 to 511, as said below
- near_source: int32 [32768], P(('gx', 'gy', 'gz')), may hold values from 0 to 511, as said below
- near_count: int32 [256], P(('gx', 'gy', 'gz')), may hold values from 42 to 128, as said below
- far_left: bfloat16 [49152, 128, 64], P(('gx', 'gy', 'gz')), may hold values from -0.5 to 0.5
- far_right: bfloat16 [49152, 128, 64], P(('gx', 'gy', 'gz')), may hold values from -0.078125 to 0.078125
- far_target: int32 [49152], P(('gx', 'gy', 'gz')), may hold values from 0 to 511, as said below
- far_source: int32 [49152], P(('gx', 'gy', 'gz')), may hold values from 0 to 511, as said below
- far_count: int32 [256], P(('gx', 'gy', 'gz')), may hold values from 64 to 192, as said below
Outputs:
- next_basis: float32 [16, 65536], P(None, ('gx', 'gy', 'gz'))
- arnoldi: float32 [16, 6], replicated
The draws below stay inside these ranges and needn't reach their ends.
Inputs may be any that keep to these rules, and one draw needn't show every extreme that they name: `near_target`: A slot on the device with gx index a and gy index c has a target cluster t with (t // 2) // 8 % 8 == c and a source cluster s with (s // 2) // 64 == a. `near_source`: as for near_target. `far_target`: as for near_target. `far_source`: as for near_target. `near_count`: some device is full and some device holds the fewest. `far_count`: some device is full and some device holds the fewest.
All inputs are finite; a program needn't handle non-finite values.
Results may differ from the reference program's by a relative error of at most 0.0039.
Values may be sent and summed in bfloat16 or wider, within the bound.
No kernel may reach another device: no remote copies, remote signals or barrier semaphores. Data moves between devices by JAX's collectives and lax.ppermute only.
A program may use at most 64 MiB of HBM per device.

```python
import jax
import jax.numpy as jnp
from jax import lax

OBJ = 16
LEAF = 128
RANK = 64
CL_DEV = 2
NEAR_DEV = 128
FAR_DEV = 192
NCL = 512
PANELS = 65536
NEAR = 32768
FAR = 49152
N_GX = 4
N_GY = 8
N_GZ = 8
DEVICES = 256


def slot_clusters(key, per_dev, by_target):
    total = per_dev * DEVICES
    slots = jnp.arange(total, dtype=jnp.int32)
    owner = slots // per_dev
    owner_gx = owner // (N_GY * N_GZ)
    owner_gy = owner // N_GZ % N_GY
    key_a, key_b, key_c, key_d, key_e = jax.random.split(key, 5)
    other_gz = jax.random.randint(key_b, (total,), 0, N_GZ, dtype=jnp.int32)
    within = jax.random.randint(key_c, (total,), 0, CL_DEV, dtype=jnp.int32)
    if by_target:
        other_gx = jax.random.randint(key_a, (total,), 0, N_GX, dtype=jnp.int32)
        group = (other_gx * N_GY + owner_gy) * N_GZ + other_gz
    else:
        spread_gy = jax.random.randint(key_a, (total,), 0, N_GY, dtype=jnp.int32)
        favored = jax.random.randint(key_d, (), 0, N_GY, dtype=jnp.int32)
        coin = jax.random.randint(key_e, (total,), 0, 4, dtype=jnp.int32)
        other_gy = jnp.where(coin == 0, favored, spread_gy).astype(jnp.int32)
        group = (owner_gx * N_GY + other_gy) * N_GZ + other_gz
    return (group * CL_DEV + within).astype(jnp.int32)


def live_counts(key, most):
    key_a, key_b = jax.random.split(key)
    counts = jax.random.randint(key_a, (DEVICES,), most // 3, most + 1, dtype=jnp.int32)
    pick = jax.random.randint(key_b, (), 0, DEVICES, dtype=jnp.int32)
    positions = jnp.arange(DEVICES, dtype=jnp.int32)
    counts = jnp.where(positions == (pick + 1) % DEVICES, most // 3, counts)
    return jnp.where(positions == pick, most, counts).astype(jnp.int32)


def draw_residual_start(key, part):
    key = jax.random.fold_in(key, 17)
    key_a, key_b = jax.random.split(key)
    offset = jax.random.uniform(key_a, (OBJ, 1), jnp.float32, 0.8, 1.6)
    noise = jnp.clip(jax.random.normal(key_b, (OBJ, PANELS), jnp.float32), -6.0, 6.0)
    return ((offset + noise) * float(PANELS) ** (-0.5)).astype(jnp.float32)


def draw_near_tiles(key, part):
    key = jax.random.fold_in(key, 18)
    spread = float(LEAF * NEAR_DEV // CL_DEV) ** (-0.5)
    unit_mean = float(CL_DEV) / float(LEAF * NEAR_DEV)
    shape = (NEAR, LEAF, LEAF)
    noise = jnp.clip(jax.random.normal(key, shape, jnp.float32), -6.0, 6.0)
    values = noise * spread + 3.0 * unit_mean
    return values.astype(jnp.bfloat16)


def draw_near_target(key, part):
    key = jax.random.fold_in(key, 11)
    return slot_clusters(key, NEAR_DEV, True)


def draw_near_source(key, part):
    key = jax.random.fold_in(key, 12)
    return slot_clusters(key, NEAR_DEV, False)


def draw_near_count(key, part):
    key = jax.random.fold_in(key, 13)
    return live_counts(key, NEAR_DEV)


def draw_far_target(key, part):
    key = jax.random.fold_in(key, 14)
    return slot_clusters(key, FAR_DEV, True)


def draw_far_source(key, part):
    key = jax.random.fold_in(key, 15)
    return slot_clusters(key, FAR_DEV, False)


def draw_far_count(key, part):
    key = jax.random.fold_in(key, 16)
    return live_counts(key, FAR_DEV)


def block_levels(key, shape, pieces, least, high):
    def one(dim, parts):
        steps = jax.random.uniform(jax.random.fold_in(jax.random.fold_in(key, 6), dim), (parts,), jnp.float32, least / len(pieces), high / len(pieces))
        return jnp.repeat(jnp.exp(steps), shape[dim] // parts).reshape((-1,) + (1,) * (len(shape) - dim - 1))

    gain = one(*pieces[0])
    for cut in pieces[1:]:
        gain = gain * one(*cut)
    return gain


def centred(key, extent, width, bound, cuts=(), held_as=jnp.bfloat16):
    array = width * jax.random.normal(key, extent, jnp.float32)
    if cuts:
        array = array * block_levels(key, extent, cuts, -0.22, 0.18)
    return jnp.clip(array, -bound, bound).astype(held_as)


def setup_inputs(seed: int = 0) -> dict:
    streams_of = jax.random.split(jax.random.key(seed), 11)
    return {
        "residual_start": draw_residual_start(jax.random.fold_in(streams_of[10], 71), 0),
        "near_tiles": draw_near_tiles(jax.random.fold_in(streams_of[10], 71), 0),
        "near_target": draw_near_target(jax.random.fold_in(streams_of[10], 71), 0),
        "near_source": draw_near_source(jax.random.fold_in(streams_of[10], 71), 0),
        "near_count": draw_near_count(jax.random.fold_in(streams_of[10], 71), 0),
        "far_left": centred(streams_of[5], (FAR, LEAF, RANK), LEAF ** -0.5, 0.5, ((0, 256),)),
        "far_right": centred(streams_of[6], (FAR, LEAF, RANK), (RANK * FAR_DEV // CL_DEV) ** -0.5, 0.078125, ((0, 256),)),
        "far_target": draw_far_target(jax.random.fold_in(streams_of[10], 71), 0),
        "far_source": draw_far_source(jax.random.fold_in(streams_of[10], 71), 0),
        "far_count": draw_far_count(jax.random.fold_in(streams_of[10], 71), 0),
    }


EPS = 1e-06

def apply_transposed(vector, near_tiles, near_target, near_source, near_count, far_left, far_right, far_target, far_source, far_count):
    rounded = vector.astype(jnp.bfloat16).reshape(OBJ, NCL, LEAF)

    def near_owner(owner, accumulated):
        offset = (owner * NEAR_DEV).astype(jnp.int32)
        blocks = lax.dynamic_slice_in_dim(near_tiles, offset, NEAR_DEV, 0).astype(jnp.float32)
        targets = lax.dynamic_slice_in_dim(near_target, offset, NEAR_DEV, 0)
        sources = lax.dynamic_slice_in_dim(near_source, offset, NEAR_DEV, 0)
        alive = (jnp.arange(NEAR_DEV, dtype=jnp.int32) < near_count[owner]).astype(jnp.float32)
        picked = jnp.take(rounded, targets, axis=1).astype(jnp.float32)
        contrib = jnp.einsum('obl,bls->obs', picked, blocks) * alive[None, :, None]
        return accumulated.at[:, sources].add(contrib)

    def far_owner(owner, accumulated):
        offset = (owner * FAR_DEV).astype(jnp.int32)
        lefts = lax.dynamic_slice_in_dim(far_left, offset, FAR_DEV, 0).astype(jnp.float32)
        rights = lax.dynamic_slice_in_dim(far_right, offset, FAR_DEV, 0).astype(jnp.float32)
        targets = lax.dynamic_slice_in_dim(far_target, offset, FAR_DEV, 0)
        sources = lax.dynamic_slice_in_dim(far_source, offset, FAR_DEV, 0)
        alive = (jnp.arange(FAR_DEV, dtype=jnp.int32) < far_count[owner]).astype(jnp.float32)
        picked = jnp.take(rounded, targets, axis=1).astype(jnp.float32)
        reduced = jnp.einsum('obl,blr->obr', picked, lefts).astype(jnp.bfloat16).astype(jnp.float32)
        contrib = jnp.einsum('obr,bsr->obs', reduced, rights) * alive[None, :, None]
        return accumulated.at[:, sources].add(contrib)
    accumulated = jnp.zeros((OBJ, NCL, LEAF), jnp.float32)
    accumulated = lax.fori_loop(0, DEVICES, near_owner, accumulated)
    accumulated = lax.fori_loop(0, DEVICES, far_owner, accumulated)
    return 0.5 * vector + accumulated.reshape(OBJ, PANELS)

def inner_rows(first, second):
    return lax.optimization_barrier(jnp.sum(first * second, axis=1))

def reference(residual_start, near_tiles, near_target, near_source, near_count, far_left, far_right, far_target, far_source, far_count):
    beta = jnp.sqrt(inner_rows(residual_start, residual_start) + EPS)
    basis_list = [residual_start / beta[:, None]]
    entries = [beta]
    for turn_index in range(2):
        image = apply_transposed(basis_list[-1], near_tiles, near_target, near_source, near_count, far_left, far_right, far_target, far_source, far_count)
        coeffs = [inner_rows(member, image) for member in basis_list]
        remainder = image
        for member, coeff in zip(basis_list, coeffs):
            remainder = remainder - coeff[:, None] * member
        length_row = jnp.sqrt(inner_rows(remainder, remainder) + EPS)
        basis_list.append(remainder / length_row[:, None])
        entries = entries + coeffs + [length_row]
    return (basis_list[-1], jnp.stack(entries, axis=1))
```

```python
import functools

import jax
import jax.numpy as jnp
from jax import lax
from jax.experimental import pallas as pl
from jax.experimental.pallas import tpu as pltpu
from jax.sharding import PartitionSpec as P

OBJ = 16
LEAF = 128
RANK = 64
CL_DEV = 2
NEAR_DEV = 128
FAR_DEV = 192
EPS = 1e-06

ALL = ("gx", "gy", "gz")
TARGETS = 64
SOURCES = 128
NEAR_CHUNK = 32
FAR_CHUNK = 48
UNROLL = 8

SMEM = pl.BlockSpec(memory_space=pltpu.SMEM)
VMEM = pl.BlockSpec(memory_space=pltpu.VMEM)
ANY = pl.BlockSpec(memory_space=pl.ANY)


def target_row(cluster):
    return (cluster >> 7) * 16 + (cluster & 15)


def source_row(cluster):
    return cluster & (SOURCES - 1)


def start_blocks(near, left, right, near_v, left_v, right_v, sems):
    copies = []
    for i in range(NEAR_DEV // NEAR_CHUNK):
        part = pl.ds(i * NEAR_CHUNK, NEAR_CHUNK)
        copies.append(pltpu.make_async_copy(near.at[part], near_v.at[part], sems.at[len(copies)]))
    for i in range(FAR_DEV // FAR_CHUNK):
        part = pl.ds(i * FAR_CHUNK, FAR_CHUNK)
        copies.append(pltpu.make_async_copy(left.at[part], left_v.at[part], sems.at[len(copies)]))
        copies.append(pltpu.make_async_copy(right.at[part], right_v.at[part], sems.at[len(copies)]))
    for copy in copies:
        copy.start()
    return copies


def multiply(copies, x, near_v, left_v, right_v, nt, ns, nc, ft, fs, fc, out):
    near_live = nc[0]
    far_live = fc[0]
    out[...] = jnp.zeros_like(out)

    def near_slot(slot):
        row = jnp.where(slot < near_live, target_row(nt[slot]), TARGETS)
        source = source_row(ns[slot])
        part = jnp.dot(x[row], near_v[slot], preferred_element_type=jnp.float32)
        return source, part

    def far_slot(slot):
        row = jnp.where(slot < far_live, target_row(ft[slot]), TARGETS)
        source = source_row(fs[slot])
        reduced = lax.dot_general(
            x[row], left_v[slot], (((1,), (1,)), ((), ())), preferred_element_type=jnp.float32
        ).astype(jnp.bfloat16)
        part = jnp.dot(reduced, right_v[slot], preferred_element_type=jnp.float32)
        return source, part

    def run(one_slot, first, live, chunk):
        groups = (jnp.clip(live - first, 0, chunk) + UNROLL - 1) // UNROLL

        def body(group, carry):
            parts = [one_slot(first + group * UNROLL + i) for i in range(UNROLL)]
            for source, part in parts:
                out[source] += part
            return carry

        lax.fori_loop(0, groups, body, 0)

    done = 0
    for i in range(NEAR_DEV // NEAR_CHUNK):
        copies[done].wait()
        done += 1
        run(near_slot, i * NEAR_CHUNK, near_live, NEAR_CHUNK)
    for i in range(FAR_DEV // FAR_CHUNK):
        copies[done].wait()
        copies[done + 1].wait()
        done += 2
        run(far_slot, i * FAR_CHUNK, far_live, FAR_CHUNK)


def first_kernel(nt, ns, nc, ft, fs, fc, beta, r, near, left, right, out, x, near_v, left_v, right_v, sems):
    copies = start_blocks(near, left, right, near_v, left_v, right_v, sems)
    x[TARGETS] = jnp.zeros((OBJ, LEAF), jnp.bfloat16)
    x[:TARGETS] = (r[...] / beta[...][None]).astype(jnp.bfloat16)
    multiply(copies, x, near_v, left_v, right_v, nt, ns, nc, ft, fs, fc, out)


def second_kernel(nt, ns, nc, ft, fs, fc, beta, h11, h21, r, image, near, left, right, out, x, near_v, left_v, right_v, sems):
    copies = start_blocks(near, left, right, near_v, left_v, right_v, sems)
    x[TARGETS] = jnp.zeros((OBJ, LEAF), jnp.bfloat16)
    basis_1 = r[...] / beta[...][None]
    basis_2 = (image[...] - h11[...][None] * basis_1) / h21[...][None]
    x[:TARGETS] = basis_2.astype(jnp.bfloat16)
    multiply(copies, x, near_v, left_v, right_v, nt, ns, nc, ft, fs, fc, out)


def product(kernel, indices, columns, fields, blocks):
    return pl.pallas_call(
        kernel,
        out_shape=jax.ShapeDtypeStruct((SOURCES, OBJ, LEAF), jnp.float32),
        in_specs=[SMEM] * 6 + [VMEM] * (len(columns) + len(fields)) + [ANY] * 3,
        out_specs=VMEM,
        scratch_shapes=[
            pltpu.VMEM((TARGETS + 1, OBJ, LEAF), jnp.bfloat16),
            pltpu.VMEM((NEAR_DEV, LEAF, LEAF), jnp.bfloat16),
            pltpu.VMEM((FAR_DEV, RANK, LEAF), jnp.bfloat16),
            pltpu.VMEM((FAR_DEV, RANK, LEAF), jnp.bfloat16),
            pltpu.SemaphoreType.DMA((NEAR_DEV // NEAR_CHUNK + 2 * (FAR_DEV // FAR_CHUNK),)),
        ],
        compiler_params=pltpu.CompilerParams(vmem_limit_bytes=56 * 1024 * 1024),
        cost_estimate=pl.CostEstimate(flops=170_000_000, bytes_accessed=12_000_000, transcendentals=0),
    )(*indices, *columns, *fields, *blocks)


def dot(first, second):
    return jnp.sum(first * second, axis=(0, 2))


def sum_gathered(value):
    for axes in (("gx", "gz"), "gy"):
        value = lax.all_gather(value, axes, axis=0, tiled=True).reshape((-1,) + value.shape).sum(0)
    return value.sum(1)


def exchange(value, axis):
    size = lax.axis_size(axis)
    total = value
    for step in range(1, size):
        total = total + lax.ppermute(value, axis, [(i, (i + step) % size) for i in range(size)])
    return total


def sum_exchanged(value):
    for axis in ("gz", "gx", "gy"):
        value = exchange(value, axis)
    return value


def sum_all_to_all(value):
    for axes in (("gx", "gz"), ("gy",)):
        size = lax.axis_size(axes)
        copies = jnp.broadcast_to(value[None], (size,) + value.shape)
        value = lax.all_to_all(copies, axes, split_axis=0, concat_axis=0).sum(0)
    return value


def scatter_sum(part, axes):
    size = lax.axis_size(axes)
    pieces = part.reshape((size, -1) + part.shape[1:])
    return lax.all_to_all(pieces, axes, split_axis=0, concat_axis=0).sum(0)


def scatter_sum_once(part):
    return scatter_sum(part, ("gy", "gz"))


def scatter_sum_twice(part):
    by_gz = jnp.swapaxes(part.reshape(8, 8, CL_DEV, OBJ, LEAF), 0, 1)
    half = scatter_sum(by_gz.reshape(8 * 8, CL_DEV, OBJ, LEAF), ("gz",))
    return scatter_sum(half, ("gy",))[0]


def guarded_square(square, whole, remainder):
    low = jnp.any(square < whole * (1.0 / 256.0))
    return lax.cond(low, lambda: lax.psum(dot(remainder, remainder), ALL), lambda: square)


def on_device(r0, near_tiles, nt, ns, nc, far_left, far_right, ft, fs, fc):
    indices = (nt, ns, nc, ft, fs, fc)
    blocks = (near_tiles, jnp.swapaxes(far_left, 1, 2), jnp.swapaxes(far_right, 1, 2))
    r = jnp.swapaxes(r0.reshape(OBJ, CL_DEV, LEAF), 0, 1)

    def spread(column):
        return jnp.broadcast_to(column[:, None], (OBJ, LEAF))

    r_targets = lax.all_gather(r, ("gx", "gz"), axis=0, tiled=True)
    square_r = sum_gathered((r * r).sum(0))
    beta = jnp.sqrt(square_r + EPS)
    basis_1 = r / beta[None, :, None]
    g11 = square_r / (square_r + EPS)

    part = product(first_kernel, indices, (spread(beta),), (r_targets,), blocks)
    image = 0.5 * basis_1 + scatter_sum_once(part)
    image_targets = lax.all_gather(image, ("gx", "gz"), axis=0, tiled=True)
    sums = sum_exchanged(jnp.stack([dot(basis_1, image), dot(image, image)]))
    h11 = sums[0]
    remainder = image - h11[None, :, None] * basis_1
    square = sums[1] - h11 * h11 * (2.0 - g11)
    square = guarded_square(square, sums[1], remainder)
    h21 = jnp.sqrt(square + EPS)
    basis_2 = remainder / h21[None, :, None]
    g12 = h11 * (1.0 - g11) / h21
    g22 = square / (square + EPS)

    part = product(
        second_kernel, indices, (spread(beta), spread(h11), spread(h21)), (r_targets, image_targets), blocks
    )
    image = 0.5 * basis_2 + scatter_sum_twice(part)
    sums = sum_all_to_all(jnp.stack([dot(basis_1, image), dot(basis_2, image), dot(image, image)]))
    h12, h22 = sums[0], sums[1]
    remainder = image - h12[None, :, None] * basis_1 - h22[None, :, None] * basis_2
    square = sums[2] - h12 * h12 * (2.0 - g11) - h22 * h22 * (2.0 - g22) + 2.0 * h12 * h22 * g12
    square = guarded_square(square, sums[2], remainder)
    h32 = jnp.sqrt(square + EPS)
    basis_3 = remainder / h32[None, :, None]
    arnoldi = jnp.stack([beta, h11, h21, h12, h22, h32], axis=1)
    return jnp.swapaxes(basis_3, 0, 1).reshape(OBJ, CL_DEV * LEAF), arnoldi


def solution(mesh):
    spread = P(ALL)
    return jax.shard_map(
        on_device,
        mesh=mesh,
        in_specs=(P(None, ALL),) + (spread,) * 9,
        out_specs=(P(None, ALL), P()),
        check_vma=False,
    )
```

```python
import functools

import jax
import jax.numpy as jnp
from jax import lax
from jax.experimental import pallas as pl
from jax.experimental.pallas import tpu as pltpu
from jax.sharding import Mesh
from jax.sharding import PartitionSpec as P

OBJ = 16
LEAF = 128
RANK = 64
CL_DEV = 2
NEAR_DEV = 128
FAR_DEV = 192
EPS = 1e-06

ALL = ("gx", "gy", "gq", "core")
PLANE = ("gx", "gq", "core")
TARGETS = 64
SOURCES = 128
NEAR_CHUNK = 32
FAR_CHUNK = 48
NEAR_STEP = 16
FAR_STEP = 16

SMEM = pl.BlockSpec(memory_space=pltpu.SMEM)
VMEM = pl.BlockSpec(memory_space=pltpu.VMEM)
HBM = pl.BlockSpec(memory_space=pltpu.HBM)


def target_row(cluster):
    return (cluster >> 7) * 16 + (cluster & 15)


def source_row(cluster, core):
    local = cluster & (SOURCES - 1)
    other = ((local >> 1) & 1) ^ core
    return other * (SOURCES // 2) + ((local >> 2) << 1) + (local & 1)


def start_blocks(near, left, right, near_v, left_v, right_v, sems):
    copies = []
    for i in range(NEAR_DEV // NEAR_CHUNK):
        part = pl.ds(i * NEAR_CHUNK, NEAR_CHUNK)
        copies.append(pltpu.make_async_copy(near.at[part], near_v.at[part], sems.at[len(copies)]))
    for i in range(FAR_DEV // FAR_CHUNK):
        part = pl.ds(i * FAR_CHUNK, FAR_CHUNK)
        copies.append(pltpu.make_async_copy(left.at[part], left_v.at[part], sems.at[len(copies)]))
        copies.append(pltpu.make_async_copy(right.at[part], right_v.at[part], sems.at[len(copies)]))
    for copy in copies:
        copy.start()
    return copies


def two_terms(value):
    high = value.astype(jnp.bfloat16)
    return high, (value - high.astype(jnp.float32)).astype(jnp.bfloat16)


def multiply(copies, field, x, near_v, left_v, right_v, nt, ns, nc, ft, fs, fc, keep, send, acc):
    core = lax.axis_index("core")
    near_live = nc[0]
    far_live = fc[0]
    high, low = two_terms(field[...])
    x[:TARGETS, :OBJ] = high
    x[:TARGETS, OBJ:] = low
    x[TARGETS] = jnp.zeros((2 * OBJ, LEAF), jnp.bfloat16)
    acc[...] = jnp.zeros_like(acc)
    own_half = lax.broadcasted_iota(jnp.int32, (2 * OBJ, LEAF), 0) // OBJ == (
        lax.broadcasted_iota(jnp.int32, (2 * OBJ, LEAF), 1) // RANK
    )

    def rows(slot, count, live, targets):
        picked = [
            x[jnp.where(slot + i < live, target_row(targets[slot + i]), TARGETS)] for i in range(count)
        ]
        return jnp.concatenate(picked, axis=0)

    def near_step(first):
        parts = []
        for i in range(0, NEAR_STEP, 2):
            slot = first + i
            pair = jnp.concatenate([near_v[slot], near_v[slot + 1]], axis=1)
            both = jnp.dot(rows(slot, 2, near_live, nt), pair, preferred_element_type=jnp.float32)
            parts.append(both[:OBJ, :LEAF] + both[OBJ : 2 * OBJ, :LEAF])
            parts.append(both[2 * OBJ : 3 * OBJ, LEAF:] + both[3 * OBJ :, LEAF:])
        for i, part in enumerate(parts):
            acc[source_row(ns[first + i], core)] += part

    def far_step(first):
        reduced = []
        for i in range(0, FAR_STEP, 4):
            slot = first + i
            lefts = left_v[pl.ds(slot, 4)].reshape(4 * RANK, LEAF)
            both = lax.dot_general(
                rows(slot, 4, far_live, ft), lefts, (((1,), (1,)), ((), ())), preferred_element_type=jnp.float32
            )
            for half in (both[: 4 * OBJ, :LEAF], both[4 * OBJ :, LEAF:]):
                pair = [half[j : j + OBJ] + half[j + OBJ : j + 2 * OBJ] for j in (0, 2 * OBJ)]
                reduced += two_terms(jnp.where(own_half, jnp.concatenate(pair, axis=0), 0.0))
        parts = []
        for i in range(0, FAR_STEP, 4):
            slot = first + i
            rights = jnp.concatenate(
                [
                    right_v[pl.ds(slot, 2)].reshape(2 * RANK, LEAF),
                    right_v[pl.ds(slot + 2, 2)].reshape(2 * RANK, LEAF),
                ],
                axis=1,
            )
            both = jnp.dot(
                jnp.concatenate(reduced[i : i + 4], axis=0), rights, preferred_element_type=jnp.float32
            )
            for half in (both[: 4 * OBJ, :LEAF], both[4 * OBJ :, LEAF:]):
                parts += [half[j : j + OBJ] + half[j + 2 * OBJ : j + 3 * OBJ] for j in (0, OBJ)]
        for i, part in enumerate(parts):
            acc[source_row(fs[first + i], core)] += part

    def run(step, size, first, live, chunk):
        groups = (jnp.clip(live - first, 0, chunk) + size - 1) // size

        def body(group, carry):
            step(first + group * size)
            return carry

        lax.fori_loop(0, groups, body, 0)

    if copies is None:
        run(near_step, NEAR_STEP, 0, near_live, NEAR_DEV)
        run(far_step, FAR_STEP, 0, far_live, FAR_DEV)
    else:
        done = 0
        for i in range(NEAR_DEV // NEAR_CHUNK):
            copies[done].wait()
            done += 1
            run(near_step, NEAR_STEP, i * NEAR_CHUNK, near_live, NEAR_CHUNK)
        for i in range(FAR_DEV // FAR_CHUNK):
            copies[done].wait()
            copies[done + 1].wait()
            done += 2
            run(far_step, FAR_STEP, i * FAR_CHUNK, far_live, FAR_CHUNK)
    keep[...] = acc[: SOURCES // 2]
    send[...] = acc[SOURCES // 2 :]


def first_kernel(nt, ns, nc, ft, fs, fc, field, near, left, right, keep, send, near_v, left_v, right_v, x, acc, sems):
    copies = start_blocks(near, left, right, near_v, left_v, right_v, sems)
    multiply(copies, field, x, near_v, left_v, right_v, nt, ns, nc, ft, fs, fc, keep, send, acc)


def second_kernel(nt, ns, nc, ft, fs, fc, field, near_v, left_v, right_v, keep, send, x, acc):
    multiply(None, field, x, near_v, left_v, right_v, nt, ns, nc, ft, fs, fc, keep, send, acc)


def product(indices, field, blocks, first):
    half = jax.ShapeDtypeStruct((SOURCES // 2, OBJ, LEAF), jnp.float32)
    scratch = [
        pltpu.VMEM((TARGETS + 1, 2 * OBJ, LEAF), jnp.bfloat16),
        pltpu.VMEM((SOURCES, OBJ, LEAF), jnp.float32),
    ]
    outs = (half, half)
    if first:
        outs += tuple(pltpu.VMEM(block.shape, block.dtype) for block in blocks)
        scratch.append(pltpu.SemaphoreType.DMA((NEAR_DEV // NEAR_CHUNK + 2 * (FAR_DEV // FAR_CHUNK),)))
    return pl.pallas_call(
        first_kernel if first else second_kernel,
        out_shape=outs,
        in_specs=[SMEM] * 6 + [VMEM] + [HBM if first else VMEM] * 3,
        out_specs=(VMEM,) * len(outs),
        scratch_shapes=scratch,
        compiler_params=pltpu.CompilerParams(vmem_limit_bytes=24 * 1024 * 1024),
        cost_estimate=pl.CostEstimate(flops=170_000_000, bytes_accessed=12_000_000, transcendentals=0),
    )(*indices, field, *blocks)


def to_all(value, axes):
    size = lax.axis_size(axes)
    return lax.all_to_all(jnp.broadcast_to(value[None], (size,) + value.shape), axes, split_axis=0, concat_axis=0)


def scatter_sum(keep, send):
    chip = keep + lax.ppermute(send, "core", [(0, 1), (1, 0)])
    pieces = chip.reshape(-1, CL_DEV, OBJ, LEAF)
    return jnp.sum(lax.all_to_all(pieces, ("gy", "gq"), split_axis=0, concat_axis=0), axis=0)


def dot(first, second):
    return jnp.sum(first * second, axis=(0, 2))


def column(value):
    return value[None, :, None]


def plainly(r, indices, blocks):
    nt, ns, nc, ft, fs, fc = indices
    near, left, right = blocks
    near_alive = (jnp.arange(NEAR_DEV, dtype=jnp.int32) < nc[0]).astype(jnp.float32)
    far_alive = (jnp.arange(FAR_DEV, dtype=jnp.int32) < fc[0]).astype(jnp.float32)

    def total(first, second):
        return lax.psum(dot(first, second), ALL)

    def apply(vector):
        gathered = lax.all_gather(vector.astype(jnp.bfloat16), PLANE, axis=0, tiled=True)
        partial = jnp.zeros((SOURCES, OBJ, LEAF), jnp.float32)
        picked = gathered[target_row(nt)]
        parts = jnp.einsum("bol,bls->bos", picked, near, preferred_element_type=jnp.float32)
        partial = partial.at[ns & (SOURCES - 1)].add(parts * near_alive[:, None, None])
        picked = gathered[target_row(ft)]
        reduced = jnp.einsum("bol,brl->bor", picked, left, preferred_element_type=jnp.float32).astype(jnp.bfloat16)
        parts = jnp.einsum("bor,brs->bos", reduced, right, preferred_element_type=jnp.float32)
        partial = partial.at[fs & (SOURCES - 1)].add(parts * far_alive[:, None, None])
        summed = lax.psum_scatter(partial, ("gy", "gq", "core"), scatter_dimension=0, tiled=True)
        return 0.5 * vector + summed

    length = jnp.sqrt(total(r, r) + EPS)
    basis = [r / column(length)]
    entries = [length]
    for _ in range(2):
        image = apply(basis[-1])
        coeffs = [total(member, image) for member in basis]
        remainder = image
        for member, coeff in zip(basis, coeffs):
            remainder = remainder - column(coeff) * member
        length = jnp.sqrt(total(remainder, remainder) + EPS)
        basis.append(remainder / column(length))
        entries += coeffs + [length]
    return basis[-1], jnp.stack(entries)


def on_device(r0, near_tiles, nt, ns, nc, far_left, far_right, ft, fs, fc):
    indices = (nt, ns, nc, ft, fs, fc)
    blocks = (near_tiles, jnp.swapaxes(far_left, 1, 2), jnp.swapaxes(far_right, 1, 2))
    r = jnp.swapaxes(r0.reshape(OBJ, CL_DEV, LEAF), 0, 1)

    r_targets = to_all(r, PLANE).reshape(TARGETS, OBJ, LEAF)
    keep, send, *held = product(indices, r_targets, blocks, True)
    u = 0.5 * r + scatter_sum(keep, send)
    u_targets = to_all(u, PLANE).reshape(TARGETS, OBJ, LEAF)
    keep, send = product(indices, u_targets, held, False)
    w = 0.5 * u + scatter_sum(keep, send)

    local = jnp.stack([dot(r, r), dot(r, u), dot(u, u), dot(r, w), dot(u, w), dot(w, w)])
    sums = jnp.sum(to_all(jnp.sum(to_all(local, PLANE), axis=0), "gy"), axis=0)
    rr, ru, uu, rw, uw, ww = (sums[i] for i in range(6))
    beta_sq = rr + EPS
    beta = jnp.sqrt(beta_sq)
    h11 = ru / beta_sq
    left_1 = (uu - 2.0 * h11 * ru + h11 * h11 * rr) / beta_sq
    h21 = jnp.sqrt(left_1 + EPS)
    scale = 1.0 / (beta * h21)
    g11 = rr / beta_sq
    g12 = (ru - h11 * rr) / beta_sq / h21
    g22 = left_1 / (left_1 + EPS)
    h12 = (rw - h11 * ru) / beta_sq / h21
    h22 = (uw - h11 * uu - h11 * (rw - h11 * ru)) * scale * scale
    image_sq = (ww - 2.0 * h11 * uw + h11 * h11 * uu) * scale * scale
    left_2 = image_sq - h12 * h12 * (2.0 - g11) - h22 * h22 * (2.0 - g22) + 2.0 * h12 * h22 * g12
    h32 = jnp.sqrt(left_2 + EPS)
    entries = jnp.stack([beta, h11, h21, h12, h22, h32])
    in_w = scale / h32
    in_u = -(h11 + h22) * in_w
    in_r = (h11 * h22 * scale - h12 / beta) / h32
    basis_3 = column(in_w) * w + column(in_u) * u + column(in_r) * r
    small = 1.0 / 1024.0
    dependent = jnp.any((left_1 * beta_sq < small * uu) | (left_2 < small * ww * scale * scale))
    basis_3, entries = lax.cond(
        dependent, lambda: plainly(r, indices, blocks), lambda: (basis_3, entries)
    )
    return jnp.swapaxes(basis_3, 0, 1).reshape(OBJ, CL_DEV * LEAF), entries.T


def solution(mesh):
    fine = Mesh(mesh.devices.reshape(4, 8, 4, 2), ALL)
    spread = P(ALL)
    return jax.shard_map(
        on_device,
        mesh=fine,
        in_specs=(P(None, ALL),) + (spread,) * 9,
        out_specs=(P(None, ALL), P()),
        check_vma=False,
    )
```

```python
import jax
import jax.numpy as jnp
from jax import lax
from jax.experimental import pallas as pl
from jax.experimental.pallas import tpu as pltpu
from jax.sharding import Mesh
from jax.sharding import PartitionSpec as P

OBJ = 16
LEAF = 128
RANK = 64
CL_DEV = 2
NEAR_DEV = 128
FAR_DEV = 192
EPS = 1e-06

ALL = ("gx", "gy", "gq", "core")
PLANE = ("gx", "gq", "core")
TARGETS = 64
SOURCES = 128
NEAR_CHUNK = 32
FAR_CHUNK = 48
NEAR_STEP = 32
FAR_STEP = 48

SCALE_R = 2.0**15
SCALE = 2.0**4
RATIO = 1.0 / 1024.0
FLOOR = 1e-5

NEAR_TARGETS = 0
NEAR_SOURCES = NEAR_TARGETS + NEAR_DEV
FAR_TARGETS = NEAR_SOURCES + NEAR_DEV
FAR_SOURCES = FAR_TARGETS + FAR_DEV

SMEM = pl.BlockSpec(memory_space=pltpu.SMEM)
VMEM = pl.BlockSpec(memory_space=pltpu.VMEM)
HBM = pl.BlockSpec(memory_space=pltpu.HBM)


def target_row(cluster):
    return (cluster >> 7) * 16 + (cluster & 15)


def source_row(cluster, core):
    local = cluster & (SOURCES - 1)
    other = ((local >> 1) & 1) ^ core
    return other * (SOURCES // 2) + ((local >> 2) << 1) + (local & 1)


def start_blocks(near, left, right, near_v, left_v, right_v, sems):
    copies = []
    for i in range(NEAR_DEV // NEAR_CHUNK):
        near_part = pl.ds(i * NEAR_CHUNK, NEAR_CHUNK)
        far_part = pl.ds(i * FAR_CHUNK, FAR_CHUNK)
        for source, held, part in ((left, left_v, far_part), (near, near_v, near_part), (right, right_v, far_part)):
            copies.append(pltpu.make_async_copy(source.at[part], held.at[part], sems.at[len(copies)]))
    for copy in copies:
        copy.start()
    return copies


def two_terms(value):
    high = value.astype(jnp.bfloat16)
    return high, (value - high.astype(jnp.float32)).astype(jnp.bfloat16)


def multiply(rows_of, live, field, near, left, right, keep, send, x, acc, near_v, left_v, right_v, sems):
    copies = start_blocks(near, left, right, near_v, left_v, right_v, sems)
    high, low = two_terms(field[...])
    x[:, :OBJ] = high
    x[:, OBJ:] = low
    acc[...] = jnp.zeros_like(acc)
    own_half = lax.broadcasted_iota(jnp.int32, (2 * OBJ, LEAF), 0) // OBJ == (
        lax.broadcasted_iota(jnp.int32, (2 * OBJ, LEAF), 1) // RANK
    )

    def rows(base, slot, count):
        return jnp.concatenate([x[rows_of[base + slot + i]] for i in range(count)], axis=0)

    def add(parts, base, slot):
        for i, part in enumerate(parts):
            acc[rows_of[base + slot + i]] += part

    def step(index):
        near_first = index * NEAR_STEP
        far_first = index * FAR_STEP
        reduced = []
        for i in range(0, FAR_STEP, 4):
            slot = far_first + i
            lefts = left_v[pl.ds(slot, 4)].reshape(4 * RANK, LEAF)
            both = lax.dot_general(
                rows(FAR_TARGETS, slot, 4), lefts, (((1,), (1,)), ((), ())), preferred_element_type=jnp.float32
            )
            for half in (both[: 4 * OBJ, :LEAF], both[4 * OBJ :, LEAF:]):
                pair = [half[j : j + OBJ] + half[j + OBJ : j + 2 * OBJ] for j in (0, 2 * OBJ)]
                reduced += two_terms(jnp.where(own_half, jnp.concatenate(pair, axis=0), 0.0))
        near_parts = []
        for i in range(0, NEAR_STEP, 2):
            slot = near_first + i
            pair = jnp.concatenate([near_v[slot], near_v[slot + 1]], axis=1)
            both = jnp.dot(rows(NEAR_TARGETS, slot, 2), pair, preferred_element_type=jnp.float32)
            near_parts.append(both[:OBJ, :LEAF] + both[OBJ : 2 * OBJ, :LEAF])
            near_parts.append(both[2 * OBJ : 3 * OBJ, LEAF:] + both[3 * OBJ :, LEAF:])
        add(near_parts, NEAR_SOURCES, near_first)
        far_parts = []
        for i in range(0, FAR_STEP, 4):
            slot = far_first + i
            rights = jnp.concatenate(
                [
                    right_v[pl.ds(slot, 2)].reshape(2 * RANK, LEAF),
                    right_v[pl.ds(slot + 2, 2)].reshape(2 * RANK, LEAF),
                ],
                axis=1,
            )
            both = jnp.dot(
                jnp.concatenate(reduced[i : i + 4], axis=0), rights, preferred_element_type=jnp.float32
            )
            for half in (both[: 4 * OBJ, :LEAF], both[4 * OBJ :, LEAF:]):
                far_parts += [half[j : j + OBJ] + half[j + 2 * OBJ : j + 3 * OBJ] for j in (0, OBJ)]
        add(far_parts, FAR_SOURCES, far_first)

    steps = jnp.maximum((live[0] + NEAR_STEP - 1) // NEAR_STEP, (live[1] + FAR_STEP - 1) // FAR_STEP)
    per_chunk = NEAR_CHUNK // NEAR_STEP
    for chunk in range(NEAR_DEV // NEAR_CHUNK):
        for copy in copies[3 * chunk : 3 * chunk + 3]:
            copy.wait()

        def body(index, carry, first=chunk * per_chunk):
            step(first + index)
            return carry

        lax.fori_loop(0, jnp.clip(steps - chunk * per_chunk, 0, per_chunk), body, 0)
    keep[...] = acc[: SOURCES // 2]
    send[...] = acc[SOURCES // 2 : SOURCES]


def product(rows_of, live, field, blocks):
    half = jax.ShapeDtypeStruct((SOURCES // 2, OBJ, LEAF), jnp.float32)
    return pl.pallas_call(
        multiply,
        out_shape=(half, half),
        in_specs=[SMEM] * 2 + [VMEM] + [HBM] * 3,
        out_specs=(VMEM, VMEM),
        scratch_shapes=[
            pltpu.VMEM((TARGETS, 2 * OBJ, LEAF), jnp.bfloat16),
            pltpu.VMEM((SOURCES + 1, OBJ, LEAF), jnp.float32),
            pltpu.VMEM((NEAR_DEV, LEAF, LEAF), jnp.bfloat16),
            pltpu.VMEM((FAR_DEV, RANK, LEAF), jnp.bfloat16),
            pltpu.VMEM((FAR_DEV, RANK, LEAF), jnp.bfloat16),
            pltpu.SemaphoreType.DMA((3 * (NEAR_DEV // NEAR_CHUNK),)),
        ],
        compiler_params=pltpu.CompilerParams(vmem_limit_bytes=24 * 1024 * 1024),
        cost_estimate=pl.CostEstimate(flops=170_000_000, bytes_accessed=12_000_000, transcendentals=0),
    )(rows_of, live, field, *blocks)


def to_all(value, axes):
    size = lax.axis_size(axes)
    return lax.all_to_all(jnp.broadcast_to(value[None], (size,) + value.shape), axes, split_axis=0, concat_axis=0)


def scatter_sum(keep, send):
    chip = keep + lax.ppermute(send, "core", [(0, 1), (1, 0)])
    pieces = (chip * SCALE).astype(jnp.float16).reshape(-1, CL_DEV, OBJ, LEAF)
    moved = lax.all_to_all(pieces, ("gy", "gq"), split_axis=0, concat_axis=0)
    return jnp.sum(moved.astype(jnp.float32), axis=0) * (1.0 / SCALE)


def gather_targets(value, scale):
    moved = to_all((value * scale).astype(jnp.float16), PLANE)
    return moved.astype(jnp.float32).reshape(TARGETS, OBJ, LEAF) * (1.0 / scale)


def dot(first, second):
    return jnp.sum(first * second, axis=(0, 2))


def column(value):
    return value[None, :, None]


def finish(sums_ref, r_ref, u_ref, w_ref, basis_ref, entries_ref, fails_ref):
    sums = jnp.sum(sums_ref[...], axis=0)
    rr, ru, uu, rw, uw, ww = (sums[i : i + 1] for i in range(6))
    beta_sq = rr + EPS
    beta = jnp.sqrt(beta_sq)
    h11 = ru / beta_sq
    left_1 = (uu - 2.0 * h11 * ru + h11 * h11 * rr) / beta_sq
    h21 = jnp.sqrt(left_1 + EPS)
    scale = 1.0 / (beta * h21)
    g11 = rr / beta_sq
    g12 = (ru - h11 * rr) / beta_sq / h21
    g22 = left_1 / (left_1 + EPS)
    h12 = (rw - h11 * ru) / beta_sq / h21
    h22 = (uw - h11 * uu - h11 * (rw - h11 * ru)) * scale * scale
    image_sq = (ww - 2.0 * h11 * uw + h11 * h11 * uu) * scale * scale
    left_2 = image_sq - h12 * h12 * (2.0 - g11) - h22 * h22 * (2.0 - g22) + 2.0 * h12 * h22 * g12
    h32 = jnp.sqrt(left_2 + EPS)
    entries_ref[...] = jnp.concatenate([beta, h11, h21, h12, h22, h32], axis=0)
    in_w = scale / h32
    in_u = -(h11 + h22) * in_w
    in_r = (h11 * h22 * scale - h12 / beta) / h32
    own = lax.broadcasted_iota(jnp.int32, (OBJ, OBJ), 0) == lax.broadcasted_iota(jnp.int32, (OBJ, OBJ), 1)

    def down(row):
        return jnp.sum(jnp.where(own, row, 0.0), axis=1, keepdims=True)

    in_w, in_u, in_r = down(in_w), down(in_u), down(in_r)
    for i in range(CL_DEV):
        lanes = pl.ds(i * LEAF, LEAF)
        basis_ref[:, lanes] = in_w * w_ref[i] + in_u * u_ref[i] + in_r * r_ref[:, lanes]
    rest_1 = left_1 * beta_sq
    rest_2 = left_2 * beta_sq * h21 * h21
    sound = (rest_1 >= RATIO * uu) & (rest_2 >= RATIO * ww) & (rest_1 >= FLOOR) & (rest_2 >= FLOOR)
    fails_ref[0] = jnp.sum(jnp.where(sound, 0.0, 1.0)).astype(jnp.int32)


def plainly(r, indices, blocks):
    nt, ns, nc, ft, fs, fc = indices
    near, left, right = blocks
    near_alive = (jnp.arange(NEAR_DEV, dtype=jnp.int32) < nc[0]).astype(jnp.float32)
    far_alive = (jnp.arange(FAR_DEV, dtype=jnp.int32) < fc[0]).astype(jnp.float32)

    def total(first, second):
        plane = jnp.sum(to_all(dot(first, second)[None], PLANE), axis=0)
        return jnp.sum(to_all(plane, "gy"), axis=0)[0]

    def apply(vector):
        gathered = to_all(vector, PLANE).reshape(TARGETS, OBJ, LEAF).astype(jnp.bfloat16)
        partial = jnp.zeros((SOURCES, OBJ, LEAF), jnp.float32)
        picked = gathered[target_row(nt)]
        parts = jnp.einsum("bol,bls->bos", picked, near, preferred_element_type=jnp.float32)
        partial = partial.at[ns & (SOURCES - 1)].add(parts * near_alive[:, None, None])
        picked = gathered[target_row(ft)]
        reduced = jnp.einsum("bol,brl->bor", picked, left, preferred_element_type=jnp.float32).astype(jnp.bfloat16)
        parts = jnp.einsum("bor,brs->bos", reduced, right, preferred_element_type=jnp.float32)
        partial = partial.at[fs & (SOURCES - 1)].add(parts * far_alive[:, None, None])
        pieces = partial.reshape(-1, CL_DEV, OBJ, LEAF)
        moved = lax.all_to_all(pieces, ("gy", "gq", "core"), split_axis=0, concat_axis=0)
        return 0.5 * vector + jnp.sum(moved, axis=0)

    length = jnp.sqrt(total(r, r) + EPS)
    basis = [r / column(length)]
    entries = [length]
    for _ in range(2):
        image = apply(basis[-1])
        coeffs = [total(member, image) for member in basis]
        remainder = image
        for member, coeff in zip(basis, coeffs):
            remainder = remainder - column(coeff) * member
        length = jnp.sqrt(total(remainder, remainder) + EPS)
        basis.append(remainder / column(length))
        entries += coeffs + [length]
    return jnp.swapaxes(basis[-1], 0, 1).reshape(OBJ, CL_DEV * LEAF), jnp.stack(entries)


def on_device(r0, near_tiles, nt, ns, nc, far_left, far_right, ft, fs, fc):
    indices = (nt, ns, nc, ft, fs, fc)
    blocks = (near_tiles, jnp.swapaxes(far_left, 1, 2), jnp.swapaxes(far_right, 1, 2))
    r = jnp.swapaxes(r0.reshape(OBJ, CL_DEV, LEAF), 0, 1)

    core = lax.axis_index("core")
    near_live = jnp.arange(NEAR_DEV, dtype=jnp.int32) < nc[0]
    far_live = jnp.arange(FAR_DEV, dtype=jnp.int32) < fc[0]
    rows_of = jnp.concatenate(
        [
            target_row(nt),
            jnp.where(near_live, source_row(ns, core), SOURCES),
            target_row(ft),
            jnp.where(far_live, source_row(fs, core), SOURCES),
        ]
    )
    live = jnp.concatenate([nc, fc])

    u = 0.5 * r + scatter_sum(*product(rows_of, live, gather_targets(r, SCALE_R), blocks))
    w = 0.5 * u + scatter_sum(*product(rows_of, live, gather_targets(u, SCALE), blocks))
    local = jnp.stack([dot(r, r), dot(r, u), dot(u, u), dot(r, w), dot(u, w), dot(w, w)])
    sums = to_all(jnp.sum(to_all(local, PLANE), axis=0), "gy")
    basis_3, entries, fails = pl.pallas_call(
        finish,
        out_shape=(
            jax.ShapeDtypeStruct((OBJ, CL_DEV * LEAF), jnp.float32),
            jax.ShapeDtypeStruct((6, OBJ), jnp.float32),
            jax.ShapeDtypeStruct((1,), jnp.int32),
        ),
        in_specs=[VMEM] * 4,
        out_specs=(VMEM, VMEM, SMEM),
    )(sums, r0, u, w)
    basis_3, entries = lax.cond(
        fails[0] == 0, lambda: (basis_3, entries), lambda: plainly(r, indices, blocks)
    )
    return basis_3, entries.T


def solution(mesh):
    fine = Mesh(mesh.devices.reshape(4, 8, 4, 2), ALL)
    spread = P(ALL)
    return jax.shard_map(
        on_device,
        mesh=fine,
        in_specs=(P(None, ALL),) + (spread,) * 9,
        out_specs=(P(None, ALL), P()),
        check_vma=False,
    )
```

```python
import jax
import jax.numpy as jnp
from jax import lax
from jax.experimental import pallas as pl
from jax.experimental.pallas import tpu as pltpu
from jax.sharding import Mesh
from jax.sharding import PartitionSpec as P

OBJ = 16
LEAF = 128
RANK = 64
CL_DEV = 2
NEAR_DEV = 128
FAR_DEV = 192
EPS = 1e-06

ALL = ("gx", "gy", "gq", "core")
PLANE = ("gx", "gq", "core")
TARGETS = 64
SOURCES = 128
NEAR_CHUNK = 32
FAR_CHUNK = 48
NEAR_STEP = 32
FAR_STEP = 48

SCALE_R = 2.0**15
SCALE = 2.0**4
RATIO = 1.0 / 1024.0
FLOOR = 1e-5

SMEM = pl.BlockSpec(memory_space=pltpu.SMEM)
VMEM = pl.BlockSpec(memory_space=pltpu.VMEM)
HBM = pl.BlockSpec(memory_space=pltpu.HBM)


def target_row(cluster):
    return (cluster >> 7) * 16 + (cluster & 15)


def start_blocks(near, left, right, near_v, left_v, right_v, sems):
    copies = []
    for i in range(NEAR_DEV // NEAR_CHUNK):
        near_part = pl.ds(i * NEAR_CHUNK, NEAR_CHUNK)
        far_part = pl.ds(i * FAR_CHUNK, FAR_CHUNK)
        for source, held, part in ((left, left_v, far_part), (near, near_v, near_part), (right, right_v, far_part)):
            copies.append(pltpu.make_async_copy(source.at[part], held.at[part], sems.at[len(copies)]))
    for copy in copies:
        copy.start()
    return copies


def two_terms(value):
    high = value.astype(jnp.bfloat16)
    return high, (value - high.astype(jnp.float32)).astype(jnp.bfloat16)


def multiply(
    nt, ns, ft, fs, nc, fc, field, near, left, right, keep, send,
    x, acc, near_v, left_v, right_v, sems, nt_s, ns_s, ft_s, fs_s, nc_s, fc_s, index_sems,
):
    fetches = [
        pltpu.make_async_copy(source, held, index_sems.at[i])
        for i, (source, held) in enumerate(
            ((nt, nt_s), (ns, ns_s), (ft, ft_s), (fs, fs_s), (nc, nc_s), (fc, fc_s))
        )
    ]
    for fetch in fetches:
        fetch.start()
    copies = start_blocks(near, left, right, near_v, left_v, right_v, sems)
    high, low = two_terms(field[...])
    x[:TARGETS, :OBJ] = high
    x[:TARGETS, OBJ:] = low
    x[TARGETS] = jnp.zeros((2 * OBJ, LEAF), jnp.bfloat16)
    acc[...] = jnp.zeros_like(acc)
    own_half = lax.broadcasted_iota(jnp.int32, (2 * OBJ, LEAF), 0) // OBJ == (
        lax.broadcasted_iota(jnp.int32, (2 * OBJ, LEAF), 1) // RANK
    )

    for fetch in fetches:
        fetch.wait()
    near_live = nc_s[0]
    far_live = fc_s[0]

    def rows(targets, live, slot, count):
        picked = [
            x[jnp.where(slot + i < live, target_row(targets[slot + i]), TARGETS)] for i in range(count)
        ]
        return jnp.concatenate(picked, axis=0)

    def add(parts, sources, slot):
        for i, part in enumerate(parts):
            acc[sources[slot + i] & (SOURCES - 1)] += part

    def step(index):
        near_first = index * NEAR_STEP
        far_first = index * FAR_STEP
        reduced = []
        for i in range(0, FAR_STEP, 4):
            slot = far_first + i
            lefts = left_v[pl.ds(slot, 4)].reshape(4 * RANK, LEAF)
            both = lax.dot_general(
                rows(ft_s, far_live, slot, 4), lefts, (((1,), (1,)), ((), ())), preferred_element_type=jnp.float32
            )
            for half in (both[: 4 * OBJ, :LEAF], both[4 * OBJ :, LEAF:]):
                pair = [half[j : j + OBJ] + half[j + OBJ : j + 2 * OBJ] for j in (0, 2 * OBJ)]
                reduced += two_terms(jnp.where(own_half, jnp.concatenate(pair, axis=0), 0.0))
        near_parts = []
        for i in range(0, NEAR_STEP, 2):
            slot = near_first + i
            pair = jnp.concatenate([near_v[slot], near_v[slot + 1]], axis=1)
            both = jnp.dot(rows(nt_s, near_live, slot, 2), pair, preferred_element_type=jnp.float32)
            near_parts.append(both[:OBJ, :LEAF] + both[OBJ : 2 * OBJ, :LEAF])
            near_parts.append(both[2 * OBJ : 3 * OBJ, LEAF:] + both[3 * OBJ :, LEAF:])
        add(near_parts, ns_s, near_first)
        far_parts = []
        for i in range(0, FAR_STEP, 4):
            slot = far_first + i
            rights = jnp.concatenate(
                [
                    right_v[pl.ds(slot, 2)].reshape(2 * RANK, LEAF),
                    right_v[pl.ds(slot + 2, 2)].reshape(2 * RANK, LEAF),
                ],
                axis=1,
            )
            both = jnp.dot(
                jnp.concatenate(reduced[i : i + 4], axis=0), rights, preferred_element_type=jnp.float32
            )
            for half in (both[: 4 * OBJ, :LEAF], both[4 * OBJ :, LEAF:]):
                far_parts += [half[j : j + OBJ] + half[j + 2 * OBJ : j + 3 * OBJ] for j in (0, OBJ)]
        add(far_parts, fs_s, far_first)

    steps = jnp.maximum((near_live + NEAR_STEP - 1) // NEAR_STEP, (far_live + FAR_STEP - 1) // FAR_STEP)
    per_chunk = NEAR_CHUNK // NEAR_STEP
    for chunk in range(NEAR_DEV // NEAR_CHUNK):
        for copy in copies[3 * chunk : 3 * chunk + 3]:
            copy.wait()

        def body(index, carry, first=chunk * per_chunk):
            step(first + index)
            return carry

        lax.fori_loop(0, jnp.clip(steps - chunk * per_chunk, 0, per_chunk), body, 0)
    core = lax.axis_index("core")
    by_core = acc.reshape(SOURCES // 4, 4, OBJ, LEAF)
    keep[...] = by_core[:, pl.ds(2 * core, 2)].reshape(keep.shape)
    send[...] = by_core[:, pl.ds(2 - 2 * core, 2)].reshape(send.shape)


def product(lists, field, blocks):
    half = jax.ShapeDtypeStruct((SOURCES // 2, OBJ, LEAF), jnp.float32)
    return pl.pallas_call(
        multiply,
        out_shape=(half, half),
        in_specs=[HBM] * 6 + [VMEM] + [HBM] * 3,
        out_specs=(VMEM, VMEM),
        scratch_shapes=[
            pltpu.VMEM((TARGETS + 1, 2 * OBJ, LEAF), jnp.bfloat16),
            pltpu.VMEM((SOURCES, OBJ, LEAF), jnp.float32),
            pltpu.VMEM((NEAR_DEV, LEAF, LEAF), jnp.bfloat16),
            pltpu.VMEM((FAR_DEV, RANK, LEAF), jnp.bfloat16),
            pltpu.VMEM((FAR_DEV, RANK, LEAF), jnp.bfloat16),
            pltpu.SemaphoreType.DMA((3 * (NEAR_DEV // NEAR_CHUNK),)),
            pltpu.SMEM((NEAR_DEV,), jnp.int32),
            pltpu.SMEM((NEAR_DEV,), jnp.int32),
            pltpu.SMEM((FAR_DEV,), jnp.int32),
            pltpu.SMEM((FAR_DEV,), jnp.int32),
            pltpu.SMEM((1,), jnp.int32),
            pltpu.SMEM((1,), jnp.int32),
            pltpu.SemaphoreType.DMA((6,)),
        ],
        compiler_params=pltpu.CompilerParams(vmem_limit_bytes=24 * 1024 * 1024),
        cost_estimate=pl.CostEstimate(flops=170_000_000, bytes_accessed=12_000_000, transcendentals=0),
    )(*lists, field, *blocks)


def to_all(value, axes):
    size = lax.axis_size(axes)
    return lax.all_to_all(jnp.broadcast_to(value[None], (size,) + value.shape), axes, split_axis=0, concat_axis=0)


def scatter_sum(keep, send):
    other = lax.ppermute((send * SCALE).astype(jnp.float16), "core", [(0, 1), (1, 0)])
    pieces = (keep * SCALE + other.astype(jnp.float32)).astype(jnp.float16).reshape(-1, CL_DEV, OBJ, LEAF)
    moved = lax.all_to_all(pieces, ("gy", "gq"), split_axis=0, concat_axis=0)
    return jnp.sum(moved.astype(jnp.float32), axis=0) * (1.0 / SCALE)


def gather_targets(value, scale):
    moved = to_all((value * scale).astype(jnp.float16), PLANE)
    return moved.astype(jnp.float32).reshape(TARGETS, OBJ, LEAF) * (1.0 / scale)


def dot(first, second):
    return jnp.sum(first * second, axis=(0, 2))


def column(value):
    return value[None, :, None]


def finish(sums_ref, r_ref, u_ref, w_ref, basis_ref, entries_ref, fails_ref):
    sums = sums_ref[...]
    rr, ru, uu, rw, uw, ww = (sums[i : i + 1] for i in range(6))
    beta_sq = rr + EPS
    beta = jnp.sqrt(beta_sq)
    h11 = ru / beta_sq
    left_1 = (uu - 2.0 * h11 * ru + h11 * h11 * rr) / beta_sq
    h21 = jnp.sqrt(left_1 + EPS)
    scale = 1.0 / (beta * h21)
    g11 = rr / beta_sq
    g12 = (ru - h11 * rr) / beta_sq / h21
    g22 = left_1 / (left_1 + EPS)
    h12 = (rw - h11 * ru) / beta_sq / h21
    h22 = (uw - h11 * uu - h11 * (rw - h11 * ru)) * scale * scale
    image_sq = (ww - 2.0 * h11 * uw + h11 * h11 * uu) * scale * scale
    left_2 = image_sq - h12 * h12 * (2.0 - g11) - h22 * h22 * (2.0 - g22) + 2.0 * h12 * h22 * g12
    h32 = jnp.sqrt(left_2 + EPS)
    entries_ref[...] = jnp.concatenate([beta, h11, h21, h12, h22, h32], axis=0)
    in_w = scale / h32
    in_u = -(h11 + h22) * in_w
    in_r = (h11 * h22 * scale - h12 / beta) / h32
    own = lax.broadcasted_iota(jnp.int32, (OBJ, OBJ), 0) == lax.broadcasted_iota(jnp.int32, (OBJ, OBJ), 1)

    def down(row):
        return jnp.sum(jnp.where(own, row, 0.0), axis=1, keepdims=True)

    in_w, in_u, in_r = down(in_w), down(in_u), down(in_r)
    for i in range(CL_DEV):
        lanes = pl.ds(i * LEAF, LEAF)
        basis_ref[:, lanes] = in_w * w_ref[i] + in_u * u_ref[i] + in_r * r_ref[:, lanes]
    rest_1 = left_1 * beta_sq
    rest_2 = left_2 * beta_sq * h21 * h21
    sound = (rest_1 >= RATIO * uu) & (rest_2 >= RATIO * ww) & (rest_1 >= FLOOR) & (rest_2 >= FLOOR)
    fails_ref[0] = jnp.sum(jnp.where(sound, 0.0, 1.0)).astype(jnp.int32)


def plainly(r0, indices, blocks):
    r = jnp.swapaxes(r0.reshape(OBJ, CL_DEV, LEAF), 0, 1)
    nt, ns, nc, ft, fs, fc = indices
    near, left, right = blocks
    near_alive = (jnp.arange(NEAR_DEV, dtype=jnp.int32) < nc[0]).astype(jnp.float32)
    far_alive = (jnp.arange(FAR_DEV, dtype=jnp.int32) < fc[0]).astype(jnp.float32)

    def total(first, second):
        plane = jnp.sum(to_all(dot(first, second)[None], PLANE), axis=0)
        return jnp.sum(to_all(plane, "gy"), axis=0)[0]

    def apply(vector):
        gathered = to_all(vector, PLANE).reshape(TARGETS, OBJ, LEAF).astype(jnp.bfloat16)
        partial = jnp.zeros((SOURCES, OBJ, LEAF), jnp.float32)
        picked = gathered[target_row(nt)]
        parts = jnp.einsum("bol,bls->bos", picked, near, preferred_element_type=jnp.float32)
        partial = partial.at[ns & (SOURCES - 1)].add(parts * near_alive[:, None, None])
        picked = gathered[target_row(ft)]
        reduced = jnp.einsum("bol,brl->bor", picked, left, preferred_element_type=jnp.float32).astype(jnp.bfloat16)
        parts = jnp.einsum("bor,brs->bos", reduced, right, preferred_element_type=jnp.float32)
        partial = partial.at[fs & (SOURCES - 1)].add(parts * far_alive[:, None, None])
        pieces = partial.reshape(-1, CL_DEV, OBJ, LEAF)
        moved = lax.all_to_all(pieces, ("gy", "gq", "core"), split_axis=0, concat_axis=0)
        return 0.5 * vector + jnp.sum(moved, axis=0)

    length = jnp.sqrt(total(r, r) + EPS)
    basis = [r / column(length)]
    entries = [length]
    for _ in range(2):
        image = apply(basis[-1])
        coeffs = [total(member, image) for member in basis]
        remainder = image
        for member, coeff in zip(basis, coeffs):
            remainder = remainder - column(coeff) * member
        length = jnp.sqrt(total(remainder, remainder) + EPS)
        basis.append(remainder / column(length))
        entries += coeffs + [length]
    return jnp.swapaxes(basis[-1], 0, 1).reshape(OBJ, CL_DEV * LEAF), jnp.stack(entries)


def on_device(r0, near_tiles, nt, ns, nc, far_left, far_right, ft, fs, fc):
    indices = (nt, ns, nc, ft, fs, fc)
    blocks = (near_tiles, jnp.swapaxes(far_left, 1, 2), jnp.swapaxes(far_right, 1, 2))
    r = jnp.swapaxes(r0.reshape(OBJ, CL_DEV, LEAF), 0, 1)

    lists = (nt, ns, ft, fs, nc, fc)
    u = 0.5 * r + scatter_sum(*product(lists, gather_targets(r, SCALE_R), blocks))
    w = 0.5 * u + scatter_sum(*product(lists, gather_targets(u, SCALE), blocks))
    local = jnp.stack([dot(r, r), dot(r, u), dot(u, u), dot(r, w), dot(u, w), dot(w, w)])
    sums = jnp.sum(to_all(local, PLANE), axis=0)
    for distance in (1, 2, 4):
        sums += lax.ppermute(sums, "gy", [(i, i ^ distance) for i in range(8)])
    basis_3, entries, fails = pl.pallas_call(
        finish,
        out_shape=(
            jax.ShapeDtypeStruct((OBJ, CL_DEV * LEAF), jnp.float32),
            jax.ShapeDtypeStruct((6, OBJ), jnp.float32),
            jax.ShapeDtypeStruct((1,), jnp.int32),
        ),
        in_specs=[VMEM] * 4,
        out_specs=(VMEM, VMEM, SMEM),
        compiler_params=pltpu.CompilerParams(vmem_limit_bytes=2 * 1024 * 1024),
    )(sums, r0, u, w)
    basis_3, entries = lax.cond(
        fails[0] == 0, lambda: (basis_3, entries), lambda: plainly(r0, indices, blocks)
    )
    return basis_3, entries.T


def solution(mesh):
    fine = Mesh(mesh.devices.reshape(4, 8, 4, 2), ALL)
    spread = P(ALL)
    return jax.shard_map(
        on_device,
        mesh=fine,
        in_specs=(P(None, ALL),) + (spread,) * 9,
        out_specs=(P(None, ALL), P()),
        check_vma=False,
    )
```

```python
import jax
import jax.numpy as jnp
from jax import lax
from jax.experimental import pallas as pl
from jax.experimental.pallas import tpu as pltpu
from jax.sharding import Mesh
from jax.sharding import PartitionSpec as P

OBJ = 16
LEAF = 128
RANK = 64
CL_DEV = 2
NEAR_DEV = 128
FAR_DEV = 192
EPS = 1e-06

ALL = ("gx", "gy", "gq", "core")
PLANE = ("gx", "gq", "core")
TARGETS = 64
SOURCES = 128
NEAR_STEP = NEAR_CHUNK = 32
FAR_STEP = FAR_CHUNK = 48

SCALE_R = 2.0**15
SCALE = 2.0**4
RATIO = 1.0 / 1024.0
FLOOR = 1e-5

SMEM = pl.BlockSpec(memory_space=pltpu.SMEM)
VMEM = pl.BlockSpec(memory_space=pltpu.VMEM)
HBM = pl.BlockSpec(memory_space=pltpu.HBM)


def target_row(cluster):
    return (cluster >> 7) * 16 + (cluster & 15)


def start_blocks(near, left, right, near_v, left_v, right_v, sems):
    copies = []
    for i in range(NEAR_DEV // NEAR_CHUNK):
        near_part = pl.ds(i * NEAR_CHUNK, NEAR_CHUNK)
        far_part = pl.ds(i * FAR_CHUNK, FAR_CHUNK)
        for source, held, part in ((left, left_v, far_part), (near, near_v, near_part), (right, right_v, far_part)):
            copies.append(pltpu.make_async_copy(source.at[part], held.at[part], sems.at[len(copies)]))
    for copy in copies:
        copy.start()
    return copies


def two_terms(value):
    high = value.astype(jnp.bfloat16)
    return high, (value - high.astype(jnp.float32)).astype(jnp.bfloat16)


def first_kernel(*refs):
    *indices, field, near, left, right, keep, send, near_v, left_v, right_v, sems = refs[:16]
    multiply(*indices, field, near_v, left_v, right_v, keep, send, *refs[16:], blocks_in=(near, left, right, sems))


def second_kernel(*refs):
    multiply(*refs)


def multiply(
    nt, ns, ft, fs, nc, fc, field, near_v, left_v, right_v, keep, send,
    x, acc, nt_s, ns_s, ft_s, fs_s, nc_s, fc_s, index_sems, blocks_in=None,
):
    fetches = [
        pltpu.make_async_copy(source, held, index_sems.at[i])
        for i, (source, held) in enumerate(
            ((nt, nt_s), (ns, ns_s), (ft, ft_s), (fs, fs_s), (nc, nc_s), (fc, fc_s))
        )
    ]
    for fetch in fetches:
        fetch.start()
    if blocks_in:
        near, left, right, sems = blocks_in
        copies = start_blocks(near, left, right, near_v, left_v, right_v, sems)
    high, low = two_terms(field[...])
    x[:TARGETS, :OBJ] = high
    x[:TARGETS, OBJ:] = low
    x[TARGETS] = jnp.zeros((2 * OBJ, LEAF), jnp.bfloat16)
    acc[...] = jnp.zeros_like(acc)
    own_half = lax.broadcasted_iota(jnp.int32, (2 * OBJ, LEAF), 0) // OBJ == (
        lax.broadcasted_iota(jnp.int32, (2 * OBJ, LEAF), 1) // RANK
    )

    for fetch in fetches:
        fetch.wait()
    near_live = nc_s[0]
    far_live = fc_s[0]

    def rows(targets, live, slot, count):
        picked = [
            x[jnp.where(slot + i < live, target_row(targets[slot + i]), TARGETS)] for i in range(count)
        ]
        return jnp.concatenate(picked, axis=0)

    def add(parts, sources, slot):
        for i, part in enumerate(parts):
            acc[sources[slot + i] & (SOURCES - 1)] += part

    def step(index):
        near_first = index * NEAR_STEP
        far_first = index * FAR_STEP
        reduced = []
        for i in range(0, FAR_STEP, 4):
            slot = far_first + i
            lefts = left_v[pl.ds(slot, 4)].reshape(4 * RANK, LEAF)
            both = lax.dot_general(
                rows(ft_s, far_live, slot, 4), lefts, (((1,), (1,)), ((), ())), preferred_element_type=jnp.float32
            )
            for half in (both[: 4 * OBJ, :LEAF], both[4 * OBJ :, LEAF:]):
                pair = [half[j : j + OBJ] + half[j + OBJ : j + 2 * OBJ] for j in (0, 2 * OBJ)]
                reduced += two_terms(jnp.where(own_half, jnp.concatenate(pair, axis=0), 0.0))
        near_parts = []
        for i in range(0, NEAR_STEP, 2):
            slot = near_first + i
            pair = jnp.concatenate([near_v[slot], near_v[slot + 1]], axis=1)
            both = jnp.dot(rows(nt_s, near_live, slot, 2), pair, preferred_element_type=jnp.float32)
            near_parts.append(both[:OBJ, :LEAF] + both[OBJ : 2 * OBJ, :LEAF])
            near_parts.append(both[2 * OBJ : 3 * OBJ, LEAF:] + both[3 * OBJ :, LEAF:])
        add(near_parts, ns_s, near_first)
        far_parts = []
        for i in range(0, FAR_STEP, 4):
            slot = far_first + i
            rights = jnp.concatenate(
                [
                    right_v[pl.ds(slot, 2)].reshape(2 * RANK, LEAF),
                    right_v[pl.ds(slot + 2, 2)].reshape(2 * RANK, LEAF),
                ],
                axis=1,
            )
            both = jnp.dot(
                jnp.concatenate(reduced[i : i + 4], axis=0), rights, preferred_element_type=jnp.float32
            )
            for half in (both[: 4 * OBJ, :LEAF], both[4 * OBJ :, LEAF:]):
                far_parts += [half[j : j + OBJ] + half[j + 2 * OBJ : j + 3 * OBJ] for j in (0, OBJ)]
        add(far_parts, fs_s, far_first)

    steps = jnp.maximum((near_live + NEAR_STEP - 1) // NEAR_STEP, (far_live + FAR_STEP - 1) // FAR_STEP)

    def body(index, carry):
        step(index)
        return carry

    if blocks_in:
        for chunk in range(NEAR_DEV // NEAR_CHUNK):
            for copy in copies[3 * chunk : 3 * chunk + 3]:
                copy.wait()
            lax.fori_loop(chunk, jnp.clip(steps, chunk, chunk + 1), body, 0)
    else:
        lax.fori_loop(0, steps, body, 0)
    core = lax.axis_index("core")
    by_core = acc.reshape(SOURCES // 4, 4, OBJ, LEAF)
    keep[...] = by_core[:, pl.ds(2 * core, 2)].reshape(keep.shape)
    send[...] = by_core[:, pl.ds(2 - 2 * core, 2)].reshape(send.shape)


def product(lists, field, blocks, first):
    half = jax.ShapeDtypeStruct((SOURCES // 2, OBJ, LEAF), jnp.float32)
    held = [pltpu.VMEM(block.shape, block.dtype) for block in blocks]
    held.append(pltpu.SemaphoreType.DMA((3 * (NEAR_DEV // NEAR_CHUNK),)))
    return pl.pallas_call(
        first_kernel if first else second_kernel,
        out_shape=(half, half),
        in_specs=[HBM] * 6 + [VMEM] + [HBM if first else VMEM] * 3,
        out_specs=(VMEM, VMEM),
        scratch_shapes=(held if first else [])
        + [
            pltpu.VMEM((TARGETS + 1, 2 * OBJ, LEAF), jnp.bfloat16),
            pltpu.VMEM((SOURCES, OBJ, LEAF), jnp.float32),
            pltpu.SMEM((NEAR_DEV,), jnp.int32),
            pltpu.SMEM((NEAR_DEV,), jnp.int32),
            pltpu.SMEM((FAR_DEV,), jnp.int32),
            pltpu.SMEM((FAR_DEV,), jnp.int32),
            pltpu.SMEM((1,), jnp.int32),
            pltpu.SMEM((1,), jnp.int32),
            pltpu.SemaphoreType.DMA((6,)),
        ],
        compiler_params=pltpu.CompilerParams(vmem_limit_bytes=24 * 1024 * 1024),
        cost_estimate=pl.CostEstimate(flops=170_000_000, bytes_accessed=12_000_000, transcendentals=0),
    )(*lists, field, *blocks)


def to_all(value, axes):
    size = lax.axis_size(axes)
    return lax.all_to_all(jnp.broadcast_to(value[None], (size,) + value.shape), axes, split_axis=0, concat_axis=0)


def scatter_sum(keep, send):
    other = lax.ppermute((send * SCALE).astype(jnp.float16), "core", [(0, 1), (1, 0)])
    pieces = (keep * SCALE + other.astype(jnp.float32)).astype(jnp.float16).reshape(-1, CL_DEV, OBJ, LEAF)
    moved = lax.all_to_all(pieces, ("gy", "gq"), split_axis=0, concat_axis=0)
    return jnp.sum(moved.astype(jnp.float32), axis=0) * (1.0 / SCALE)


def gather_targets(value, scale):
    moved = to_all((value * scale).astype(jnp.float16), PLANE)
    return moved.astype(jnp.float32).reshape(TARGETS, OBJ, LEAF) * (1.0 / scale)


def dot(first, second):
    return jnp.sum(first * second, axis=(0, 2))


def column(value):
    return value[None, :, None]


def finish(sums_ref, r_ref, u_ref, w_ref, basis_ref, entries_ref, fails_ref):
    sums = jnp.sum(sums_ref[...], axis=0)
    rr, ru, uu, rw, uw, ww = (sums[i : i + 1] for i in range(6))
    beta_sq = rr + EPS
    beta = jnp.sqrt(beta_sq)
    h11 = ru / beta_sq
    left_1 = (uu - 2.0 * h11 * ru + h11 * h11 * rr) / beta_sq
    h21 = jnp.sqrt(left_1 + EPS)
    scale = 1.0 / (beta * h21)
    g11 = rr / beta_sq
    g12 = (ru - h11 * rr) / beta_sq / h21
    g22 = left_1 / (left_1 + EPS)
    h12 = (rw - h11 * ru) / beta_sq / h21
    h22 = (uw - h11 * uu - h11 * (rw - h11 * ru)) * scale * scale
    image_sq = (ww - 2.0 * h11 * uw + h11 * h11 * uu) * scale * scale
    left_2 = image_sq - h12 * h12 * (2.0 - g11) - h22 * h22 * (2.0 - g22) + 2.0 * h12 * h22 * g12
    h32 = jnp.sqrt(left_2 + EPS)
    entries_ref[...] = jnp.concatenate([beta, h11, h21, h12, h22, h32], axis=0)
    in_w = scale / h32
    in_u = -(h11 + h22) * in_w
    in_r = (h11 * h22 * scale - h12 / beta) / h32
    own = lax.broadcasted_iota(jnp.int32, (OBJ, OBJ), 0) == lax.broadcasted_iota(jnp.int32, (OBJ, OBJ), 1)

    def down(row):
        return jnp.sum(jnp.where(own, row, 0.0), axis=1, keepdims=True)

    in_w, in_u, in_r = down(in_w), down(in_u), down(in_r)
    for i in range(CL_DEV):
        lanes = pl.ds(i * LEAF, LEAF)
        basis_ref[:, lanes] = in_w * w_ref[i] + in_u * u_ref[i] + in_r * r_ref[:, lanes]
    rest_1 = left_1 * beta_sq
    rest_2 = left_2 * beta_sq * h21 * h21
    sound = (rest_1 >= RATIO * uu) & (rest_2 >= RATIO * ww) & (rest_1 >= FLOOR) & (rest_2 >= FLOOR)
    fails_ref[0] = jnp.sum(jnp.where(sound, 0.0, 1.0)).astype(jnp.int32)


def plainly(r0, indices, blocks):
    r = jnp.swapaxes(r0.reshape(OBJ, CL_DEV, LEAF), 0, 1)
    nt, ns, nc, ft, fs, fc = indices
    near, left, right = blocks
    near_alive = (jnp.arange(NEAR_DEV, dtype=jnp.int32) < nc[0]).astype(jnp.float32)
    far_alive = (jnp.arange(FAR_DEV, dtype=jnp.int32) < fc[0]).astype(jnp.float32)

    def total(first, second):
        plane = jnp.sum(to_all(dot(first, second)[None], PLANE), axis=0)
        return jnp.sum(to_all(plane, "gy"), axis=0)[0]

    def apply(vector):
        gathered = to_all(vector, PLANE).reshape(TARGETS, OBJ, LEAF).astype(jnp.bfloat16)
        partial = jnp.zeros((SOURCES, OBJ, LEAF), jnp.float32)
        picked = gathered[target_row(nt)]
        parts = jnp.einsum("bol,bls->bos", picked, near, preferred_element_type=jnp.float32)
        partial = partial.at[ns & (SOURCES - 1)].add(parts * near_alive[:, None, None])
        picked = gathered[target_row(ft)]
        reduced = jnp.einsum("bol,brl->bor", picked, left, preferred_element_type=jnp.float32).astype(jnp.bfloat16)
        parts = jnp.einsum("bor,brs->bos", reduced, right, preferred_element_type=jnp.float32)
        partial = partial.at[fs & (SOURCES - 1)].add(parts * far_alive[:, None, None])
        pieces = partial.reshape(-1, CL_DEV, OBJ, LEAF)
        moved = lax.all_to_all(pieces, ("gy", "gq", "core"), split_axis=0, concat_axis=0)
        return 0.5 * vector + jnp.sum(moved, axis=0)

    length = jnp.sqrt(total(r, r) + EPS)
    basis = [r / column(length)]
    entries = [length]
    for _ in range(2):
        image = apply(basis[-1])
        coeffs = [total(member, image) for member in basis]
        remainder = image
        for member, coeff in zip(basis, coeffs):
            remainder = remainder - column(coeff) * member
        length = jnp.sqrt(total(remainder, remainder) + EPS)
        basis.append(remainder / column(length))
        entries += coeffs + [length]
    return jnp.swapaxes(basis[-1], 0, 1).reshape(OBJ, CL_DEV * LEAF), jnp.stack(entries)


def on_device(r0, near_tiles, nt, ns, nc, far_left, far_right, ft, fs, fc):
    indices = (nt, ns, nc, ft, fs, fc)
    blocks = (near_tiles, jnp.swapaxes(far_left, 1, 2), jnp.swapaxes(far_right, 1, 2))
    r = jnp.swapaxes(r0.reshape(OBJ, CL_DEV, LEAF), 0, 1)

    lists = (nt, ns, ft, fs, nc, fc)
    u = 0.5 * r + scatter_sum(*product(lists, gather_targets(r, SCALE_R), blocks, True))
    w = 0.5 * u + scatter_sum(*product(lists, gather_targets(u, SCALE), blocks, False))
    local = jnp.stack([dot(r, r), dot(r, u), dot(u, u), dot(r, w), dot(u, w), dot(w, w)])
    sums = to_all(jnp.sum(to_all(local, PLANE), axis=0), "gy")
    basis_3, entries, fails = pl.pallas_call(
        finish,
        out_shape=(
            jax.ShapeDtypeStruct((OBJ, CL_DEV * LEAF), jnp.float32),
            jax.ShapeDtypeStruct((6, OBJ), jnp.float32),
            jax.ShapeDtypeStruct((1,), jnp.int32),
        ),
        in_specs=[VMEM] * 4,
        out_specs=(VMEM, VMEM, SMEM),
        compiler_params=pltpu.CompilerParams(vmem_limit_bytes=2 * 1024 * 1024),
    )(sums, r0, u, w)
    basis_3, entries = lax.cond(
        fails[0] == 0, lambda: (basis_3, entries), lambda: plainly(r0, indices, blocks)
    )
    return basis_3, entries.T


def solution(mesh):
    fine = Mesh(mesh.devices.reshape(4, 8, 4, 2), ALL)
    spread = P(ALL)
    return jax.shard_map(
        on_device,
        mesh=fine,
        in_specs=(P(None, ALL),) + (spread,) * 9,
        out_specs=(P(None, ALL), P()),
        check_vma=False,
    )
```

```python
import jax
import jax.numpy as jnp
from jax import lax
from jax.experimental import pallas as pl
from jax.experimental.pallas import tpu as pltpu
from jax.sharding import Mesh
from jax.sharding import PartitionSpec as P

OBJ = 16
LEAF = 128
RANK = 64
CL_DEV = 2
NEAR_DEV = 128
FAR_DEV = 192
EPS = 1e-06

ALL = ("gx", "gy", "gq", "core")
PLANE = ("gx", "gq", "core")
TARGETS = 64
SOURCES = 128
NEAR_STEP = NEAR_CHUNK = 32
FAR_STEP = FAR_CHUNK = 48

SCALE_R = 2.0**15
SCALE = 2.0**4
RATIO = 1.0 / 1024.0
FLOOR = 1e-5

SMEM = pl.BlockSpec(memory_space=pltpu.SMEM)
VMEM = pl.BlockSpec(memory_space=pltpu.VMEM)
HBM = pl.BlockSpec(memory_space=pltpu.HBM)


def target_row(cluster):
    return (cluster >> 7) * 16 + (cluster & 15)


def start_blocks(near, left, right, near_v, left_v, right_v, sems):
    copies = []
    for i in range(NEAR_DEV // NEAR_CHUNK):
        near_part = pl.ds(i * NEAR_CHUNK, NEAR_CHUNK)
        far_part = pl.ds(i * FAR_CHUNK, FAR_CHUNK)
        for source, held, part in ((left, left_v, far_part), (near, near_v, near_part), (right, right_v, far_part)):
            copies.append(pltpu.make_async_copy(source.at[part], held.at[part], sems.at[len(copies)]))
    for copy in copies:
        copy.start()
    return copies


def two_terms(value):
    high = value.astype(jnp.bfloat16)
    return high, (value - high.astype(jnp.float32)).astype(jnp.bfloat16)


def first_kernel(*refs):
    *indices, field, near, left, right, keep, send, near_v, left_v, right_v, sems = refs[:16]
    multiply(*indices, field, near_v, left_v, right_v, keep, send, *refs[16:], blocks_in=(near, left, right, sems))


def second_kernel(*refs):
    multiply(*refs)


def multiply(
    nt, ns, ft, fs, nc, fc, field, near_v, left_v, right_v, keep, send,
    x, acc, nt_s, ns_s, ft_s, fs_s, nc_s, fc_s, index_sems, blocks_in=None,
):
    fetches = [
        pltpu.make_async_copy(source, held, index_sems.at[i])
        for i, (source, held) in enumerate(
            ((nt, nt_s), (ns, ns_s), (ft, ft_s), (fs, fs_s), (nc, nc_s), (fc, fc_s))
        )
    ]
    for fetch in fetches:
        fetch.start()
    if blocks_in:
        near, left, right, sems = blocks_in
        copies = start_blocks(near, left, right, near_v, left_v, right_v, sems)
    high, low = two_terms(field[...])
    x[:TARGETS, :OBJ] = high
    x[:TARGETS, OBJ:] = low
    x[TARGETS] = jnp.zeros((2 * OBJ, LEAF), jnp.bfloat16)
    acc[...] = jnp.zeros_like(acc)
    own_half = lax.broadcasted_iota(jnp.int32, (2 * OBJ, LEAF), 0) // OBJ == (
        lax.broadcasted_iota(jnp.int32, (2 * OBJ, LEAF), 1) // RANK
    )

    for fetch in fetches:
        fetch.wait()
    near_live = nc_s[0]
    far_live = fc_s[0]

    def rows(targets, live, slot, count):
        picked = [
            x[jnp.where(slot + i < live, target_row(targets[slot + i]), TARGETS)] for i in range(count)
        ]
        return jnp.concatenate(picked, axis=0)

    def add(parts, sources, slot):
        for i, part in enumerate(parts):
            acc[sources[slot + i] & (SOURCES - 1)] += part

    def step(index):
        near_first = index * NEAR_STEP
        far_first = index * FAR_STEP
        reduced = []
        for i in range(0, FAR_STEP, 4):
            slot = far_first + i
            lefts = left_v[pl.ds(slot, 4)].reshape(4 * RANK, LEAF)
            both = lax.dot_general(
                rows(ft_s, far_live, slot, 4), lefts, (((1,), (1,)), ((), ())), preferred_element_type=jnp.float32
            )
            for half in (both[: 4 * OBJ, :LEAF], both[4 * OBJ :, LEAF:]):
                pair = [half[j : j + OBJ] + half[j + OBJ : j + 2 * OBJ] for j in (0, 2 * OBJ)]
                reduced += two_terms(jnp.where(own_half, jnp.concatenate(pair, axis=0), 0.0))
        near_parts = []
        for i in range(0, NEAR_STEP, 2):
            slot = near_first + i
            pair = jnp.concatenate([near_v[slot], near_v[slot + 1]], axis=1)
            both = jnp.dot(rows(nt_s, near_live, slot, 2), pair, preferred_element_type=jnp.float32)
            near_parts.append(both[:OBJ, :LEAF] + both[OBJ : 2 * OBJ, :LEAF])
            near_parts.append(both[2 * OBJ : 3 * OBJ, LEAF:] + both[3 * OBJ :, LEAF:])
        add(near_parts, ns_s, near_first)
        far_parts = []
        for i in range(0, FAR_STEP, 4):
            slot = far_first + i
            rights = jnp.concatenate(
                [
                    right_v[pl.ds(slot, 2)].reshape(2 * RANK, LEAF),
                    right_v[pl.ds(slot + 2, 2)].reshape(2 * RANK, LEAF),
                ],
                axis=1,
            )
            both = jnp.dot(
                jnp.concatenate(reduced[i : i + 4], axis=0), rights, preferred_element_type=jnp.float32
            )
            for half in (both[: 4 * OBJ, :LEAF], both[4 * OBJ :, LEAF:]):
                far_parts += [half[j : j + OBJ] + half[j + 2 * OBJ : j + 3 * OBJ] for j in (0, OBJ)]
        add(far_parts, fs_s, far_first)

    steps = jnp.maximum((near_live + NEAR_STEP - 1) // NEAR_STEP, (far_live + FAR_STEP - 1) // FAR_STEP)

    def body(index, carry):
        step(index)
        return carry

    if blocks_in:
        for chunk in range(NEAR_DEV // NEAR_CHUNK):
            for copy in copies[3 * chunk : 3 * chunk + 3]:
                copy.wait()
            lax.fori_loop(chunk, jnp.clip(steps, chunk, chunk + 1), body, 0)
    else:
        lax.fori_loop(0, steps, body, 0)
    core = lax.axis_index("core")
    by_core = acc.reshape(SOURCES // 4, 4, OBJ, LEAF)
    keep[...] = by_core[:, pl.ds(2 * core, 2)].reshape(keep.shape)
    send[...] = by_core[:, pl.ds(2 - 2 * core, 2)].reshape(send.shape)


def product(lists, field, blocks, first):
    half = jax.ShapeDtypeStruct((SOURCES // 2, OBJ, LEAF), jnp.float32)
    held = [pltpu.VMEM(block.shape, block.dtype) for block in blocks]
    held.append(pltpu.SemaphoreType.DMA((3 * (NEAR_DEV // NEAR_CHUNK),)))
    return pl.pallas_call(
        first_kernel if first else second_kernel,
        out_shape=(half, half),
        in_specs=[HBM] * 6 + [VMEM] + [HBM if first else VMEM] * 3,
        out_specs=(VMEM, VMEM),
        scratch_shapes=(held if first else [])
        + [
            pltpu.VMEM((TARGETS + 1, 2 * OBJ, LEAF), jnp.bfloat16),
            pltpu.VMEM((SOURCES, OBJ, LEAF), jnp.float32),
            pltpu.SMEM((NEAR_DEV,), jnp.int32),
            pltpu.SMEM((NEAR_DEV,), jnp.int32),
            pltpu.SMEM((FAR_DEV,), jnp.int32),
            pltpu.SMEM((FAR_DEV,), jnp.int32),
            pltpu.SMEM((1,), jnp.int32),
            pltpu.SMEM((1,), jnp.int32),
            pltpu.SemaphoreType.DMA((6,)),
        ],
        compiler_params=pltpu.CompilerParams(vmem_limit_bytes=24 * 1024 * 1024),
        cost_estimate=pl.CostEstimate(flops=170_000_000, bytes_accessed=12_000_000, transcendentals=0),
    )(*lists, field, *blocks)


def to_all(value, axes):
    size = lax.axis_size(axes)
    return lax.all_to_all(jnp.broadcast_to(value[None], (size,) + value.shape), axes, split_axis=0, concat_axis=0)


def scatter_sum(keep, send):
    other = lax.ppermute((send * SCALE).astype(jnp.float16), "core", [(0, 1), (1, 0)])
    pieces = (keep * SCALE + other.astype(jnp.float32)).astype(jnp.float16).reshape(-1, CL_DEV, OBJ, LEAF)
    moved = lax.all_to_all(pieces, ("gy", "gq"), split_axis=0, concat_axis=0)
    return jnp.sum(moved.astype(jnp.float32), axis=0) * (1.0 / SCALE)


def gather_targets(value, scale):
    moved = to_all((value * scale).astype(jnp.float16), PLANE)
    return moved.astype(jnp.float32).reshape(TARGETS, OBJ, LEAF) * (1.0 / scale)


def dot(first, second):
    return jnp.sum(first * second, axis=(0, 2))


def column(value):
    return value[None, :, None]


def finish(sums_ref, r_ref, u_ref, applied_ref, basis_ref, entries_ref, fails_ref):
    sums = sums_ref[...]
    rr, ru, uu, rw, uw, ww = (sums[:, i * OBJ : (i + 1) * OBJ] for i in range(6))
    beta_sq = rr + EPS
    beta = jnp.sqrt(beta_sq)
    h11 = ru / beta_sq
    left_1 = (uu - 2.0 * h11 * ru + h11 * h11 * rr) / beta_sq
    h21 = jnp.sqrt(left_1 + EPS)
    scale = 1.0 / (beta * h21)
    g11 = rr / beta_sq
    g12 = (ru - h11 * rr) / beta_sq / h21
    g22 = left_1 / (left_1 + EPS)
    h12 = (rw - h11 * ru) / beta_sq / h21
    h22 = (uw - h11 * uu - h11 * (rw - h11 * ru)) * scale * scale
    image_sq = (ww - 2.0 * h11 * uw + h11 * h11 * uu) * scale * scale
    left_2 = image_sq - h12 * h12 * (2.0 - g11) - h22 * h22 * (2.0 - g22) + 2.0 * h12 * h22 * g12
    h32 = jnp.sqrt(left_2 + EPS)
    entries_ref[...] = jnp.concatenate([beta, h11, h21, h12, h22, h32], axis=0)
    in_w = scale / h32
    in_u = -(h11 + h22) * in_w
    in_r = (h11 * h22 * scale - h12 / beta) / h32
    own = lax.broadcasted_iota(jnp.int32, (OBJ, OBJ), 0) == lax.broadcasted_iota(jnp.int32, (OBJ, OBJ), 1)

    def down(row):
        return jnp.sum(jnp.where(own, row, 0.0), axis=1, keepdims=True)

    in_w, in_u, in_r = down(in_w), down(in_u), down(in_r)
    for i in range(CL_DEV):
        lanes = pl.ds(i * LEAF, LEAF)
        w = 0.5 * u_ref[i] + applied_ref[i]
        basis_ref[:, lanes] = in_w * w + in_u * u_ref[i] + in_r * r_ref[:, lanes]
    rest_1 = left_1 * beta_sq
    rest_2 = left_2 * beta_sq * h21 * h21
    sound = (rest_1 >= RATIO * uu) & (rest_2 >= RATIO * ww) & (rest_1 >= FLOOR) & (rest_2 >= FLOOR)
    fails_ref[0] = jnp.sum(jnp.where(sound, 0.0, 1.0)).astype(jnp.int32)


def plainly(r0, indices, blocks):
    r = jnp.swapaxes(r0.reshape(OBJ, CL_DEV, LEAF), 0, 1)
    nt, ns, nc, ft, fs, fc = indices
    near, left, right = blocks
    near_alive = (jnp.arange(NEAR_DEV, dtype=jnp.int32) < nc[0]).astype(jnp.float32)
    far_alive = (jnp.arange(FAR_DEV, dtype=jnp.int32) < fc[0]).astype(jnp.float32)

    def total(first, second):
        plane = jnp.sum(to_all(dot(first, second)[None], PLANE), axis=0)
        return jnp.sum(to_all(plane, "gy"), axis=0)[0]

    def apply(vector):
        gathered = to_all(vector, PLANE).reshape(TARGETS, OBJ, LEAF).astype(jnp.bfloat16)
        partial = jnp.zeros((SOURCES, OBJ, LEAF), jnp.float32)
        picked = gathered[target_row(nt)]
        parts = jnp.einsum("bol,bls->bos", picked, near, preferred_element_type=jnp.float32)
        partial = partial.at[ns & (SOURCES - 1)].add(parts * near_alive[:, None, None])
        picked = gathered[target_row(ft)]
        reduced = jnp.einsum("bol,brl->bor", picked, left, preferred_element_type=jnp.float32).astype(jnp.bfloat16)
        parts = jnp.einsum("bor,brs->bos", reduced, right, preferred_element_type=jnp.float32)
        partial = partial.at[fs & (SOURCES - 1)].add(parts * far_alive[:, None, None])
        pieces = partial.reshape(-1, CL_DEV, OBJ, LEAF)
        moved = lax.all_to_all(pieces, ("gy", "gq", "core"), split_axis=0, concat_axis=0)
        return 0.5 * vector + jnp.sum(moved, axis=0)

    length = jnp.sqrt(total(r, r) + EPS)
    basis = [r / column(length)]
    entries = [length]
    for _ in range(2):
        image = apply(basis[-1])
        coeffs = [total(member, image) for member in basis]
        remainder = image
        for member, coeff in zip(basis, coeffs):
            remainder = remainder - column(coeff) * member
        length = jnp.sqrt(total(remainder, remainder) + EPS)
        basis.append(remainder / column(length))
        entries += coeffs + [length]
    return jnp.swapaxes(basis[-1], 0, 1).reshape(OBJ, CL_DEV * LEAF), jnp.stack(entries)


def on_device(r0, near_tiles, nt, ns, nc, far_left, far_right, ft, fs, fc):
    indices = (nt, ns, nc, ft, fs, fc)
    blocks = (near_tiles, jnp.swapaxes(far_left, 1, 2), jnp.swapaxes(far_right, 1, 2))
    r = jnp.swapaxes(r0.reshape(OBJ, CL_DEV, LEAF), 0, 1)

    lists = (nt, ns, ft, fs, nc, fc)
    u = 0.5 * r + scatter_sum(*product(lists, gather_targets(r, SCALE_R), blocks, True))
    applied = scatter_sum(*product(lists, gather_targets(u, SCALE), blocks, False))
    w = 0.5 * u + applied
    dots = [dot(r, r), dot(r, u), dot(u, u), dot(r, w), dot(u, w), dot(w, w)]
    local = jnp.concatenate(dots + [jnp.zeros((LEAF - len(dots) * OBJ,), jnp.float32)])[None]
    chip = local + lax.ppermute(local, "core", [(0, 1), (1, 0)])
    sums = jnp.sum(to_all(chip, ("gx", "gy", "gq")), axis=0)
    basis_3, entries, fails = pl.pallas_call(
        finish,
        out_shape=(
            jax.ShapeDtypeStruct((OBJ, CL_DEV * LEAF), jnp.float32),
            jax.ShapeDtypeStruct((6, OBJ), jnp.float32),
            jax.ShapeDtypeStruct((1,), jnp.int32),
        ),
        in_specs=[VMEM] * 4,
        out_specs=(VMEM, VMEM, SMEM),
        compiler_params=pltpu.CompilerParams(vmem_limit_bytes=2 * 1024 * 1024),
    )(sums, r0, u, applied)
    basis_3, entries = lax.switch(
        fails[0], (lambda: (basis_3, entries), lambda: plainly(r0, indices, blocks))
    )
    return basis_3, entries.T


def solution(mesh):
    fine = Mesh(mesh.devices.reshape(4, 8, 4, 2), ALL)
    spread = P(ALL)
    return jax.shard_map(
        on_device,
        mesh=fine,
        in_specs=(P(None, ALL),) + (spread,) * 9,
        out_specs=(P(None, ALL), P()),
        check_vma=False,
    )
```

```python
import jax
import jax.numpy as jnp
from jax import lax
from jax.experimental import pallas as pl
from jax.experimental.pallas import tpu as pltpu
from jax.sharding import Mesh
from jax.sharding import PartitionSpec as P

OBJ = 16
LEAF = 128
RANK = 64
CL_DEV = 2
NEAR_DEV = 128
FAR_DEV = 192
EPS = 1e-06

ALL = ("gx", "gy", "gq", "core")
PLANE = ("gx", "gq", "core")
TARGETS = 64
SOURCES = 128
NEAR_STEP = NEAR_CHUNK = 32
FAR_STEP = FAR_CHUNK = 48

SCALE_R = 2.0**15
SCALE = 2.0**4
RATIO = 1.0 / 1024.0
FLOOR = 1e-5

SMEM = pl.BlockSpec(memory_space=pltpu.SMEM)
VMEM = pl.BlockSpec(memory_space=pltpu.VMEM)
HBM = pl.BlockSpec(memory_space=pltpu.HBM)


def target_row(cluster):
    return (cluster >> 7) * 16 + (cluster & 15)


def start_blocks(near, left, right, near_v, left_v, right_v, sems):
    copies = []
    for i in range(NEAR_DEV // NEAR_CHUNK):
        near_part = pl.ds(i * NEAR_CHUNK, NEAR_CHUNK)
        far_part = pl.ds(i * FAR_CHUNK, FAR_CHUNK)
        for source, held, part in ((left, left_v, far_part), (near, near_v, near_part), (right, right_v, far_part)):
            copies.append(pltpu.make_async_copy(source.at[part], held.at[part], sems.at[len(copies)]))
    for copy in copies:
        copy.start()
    return copies


def two_terms(value):
    high = value.astype(jnp.bfloat16)
    return high, (value - high.astype(jnp.float32)).astype(jnp.bfloat16)


def first_kernel(*refs):
    *indices, field, near, left, right, keep, send, near_v, left_v, right_v, sems = refs[:16]
    multiply(*indices, field, near_v, left_v, right_v, keep, send, *refs[16:], blocks_in=(near, left, right, sems))


def second_kernel(*refs):
    multiply(*refs)


def multiply(
    nt, ns, ft, fs, nc, fc, field, near_v, left_v, right_v, keep, send,
    x, acc, nt_s, ns_s, ft_s, fs_s, nc_s, fc_s, index_sems, blocks_in=None,
):
    fetches = [
        pltpu.make_async_copy(source, held, index_sems.at[i])
        for i, (source, held) in enumerate(
            ((nt, nt_s), (ns, ns_s), (ft, ft_s), (fs, fs_s), (nc, nc_s), (fc, fc_s))
        )
    ]
    for fetch in fetches:
        fetch.start()
    if blocks_in:
        near, left, right, sems = blocks_in
        copies = start_blocks(near, left, right, near_v, left_v, right_v, sems)
    high, low = two_terms(field[...])
    x[:TARGETS, :OBJ] = high
    x[:TARGETS, OBJ:] = low
    x[TARGETS] = jnp.zeros((2 * OBJ, LEAF), jnp.bfloat16)
    acc[...] = jnp.zeros_like(acc)
    own_half = lax.broadcasted_iota(jnp.int32, (2 * OBJ, LEAF), 0) // OBJ == (
        lax.broadcasted_iota(jnp.int32, (2 * OBJ, LEAF), 1) // RANK
    )

    for fetch in fetches:
        fetch.wait()
    near_live = nc_s[0]
    far_live = fc_s[0]

    def rows(targets, live, slot, count):
        picked = [
            x[jnp.where(slot + i < live, target_row(targets[slot + i]), TARGETS)] for i in range(count)
        ]
        return jnp.concatenate(picked, axis=0)

    def add(parts, sources, slot):
        for i, part in enumerate(parts):
            acc[sources[slot + i] & (SOURCES - 1)] += part

    def step(index):
        near_first = index * NEAR_STEP
        far_first = index * FAR_STEP
        reduced = []
        for i in range(0, FAR_STEP, 4):
            slot = far_first + i
            lefts = left_v[pl.ds(slot, 4)].reshape(4 * RANK, LEAF)
            both = lax.dot_general(
                rows(ft_s, far_live, slot, 4), lefts, (((1,), (1,)), ((), ())), preferred_element_type=jnp.float32
            )
            for half in (both[: 4 * OBJ, :LEAF], both[4 * OBJ :, LEAF:]):
                pair = [half[j : j + OBJ] + half[j + OBJ : j + 2 * OBJ] for j in (0, 2 * OBJ)]
                reduced += two_terms(jnp.where(own_half, jnp.concatenate(pair, axis=0), 0.0))
        near_parts = []
        for i in range(0, NEAR_STEP, 2):
            slot = near_first + i
            pair = jnp.concatenate([near_v[slot], near_v[slot + 1]], axis=1)
            both = jnp.dot(rows(nt_s, near_live, slot, 2), pair, preferred_element_type=jnp.float32)
            near_parts.append(both[:OBJ, :LEAF] + both[OBJ : 2 * OBJ, :LEAF])
            near_parts.append(both[2 * OBJ : 3 * OBJ, LEAF:] + both[3 * OBJ :, LEAF:])
        add(near_parts, ns_s, near_first)
        far_parts = []
        for i in range(0, FAR_STEP, 4):
            slot = far_first + i
            rights = jnp.concatenate(
                [
                    right_v[pl.ds(slot, 2)].reshape(2 * RANK, LEAF),
                    right_v[pl.ds(slot + 2, 2)].reshape(2 * RANK, LEAF),
                ],
                axis=1,
            )
            both = jnp.dot(
                jnp.concatenate(reduced[i : i + 4], axis=0), rights, preferred_element_type=jnp.float32
            )
            for half in (both[: 4 * OBJ, :LEAF], both[4 * OBJ :, LEAF:]):
                far_parts += [half[j : j + OBJ] + half[j + 2 * OBJ : j + 3 * OBJ] for j in (0, OBJ)]
        add(far_parts, fs_s, far_first)

    steps = jnp.maximum((near_live + NEAR_STEP - 1) // NEAR_STEP, (far_live + FAR_STEP - 1) // FAR_STEP)

    def body(index, carry):
        step(index)
        return carry

    if blocks_in:
        for chunk in range(NEAR_DEV // NEAR_CHUNK):
            for copy in copies[3 * chunk : 3 * chunk + 3]:
                copy.wait()
            lax.fori_loop(chunk, jnp.clip(steps, chunk, chunk + 1), body, 0)
    else:
        lax.fori_loop(0, steps, body, 0)
    core = lax.axis_index("core")
    by_core = acc.reshape(SOURCES // 4, 4, OBJ, LEAF)
    keep[...] = by_core[:, pl.ds(2 * core, 2)].reshape(keep.shape)
    send[...] = by_core[:, pl.ds(2 - 2 * core, 2)].reshape(send.shape)


def product(lists, field, blocks, first):
    half = jax.ShapeDtypeStruct((SOURCES // 2, OBJ, LEAF), jnp.float32)
    held = [pltpu.VMEM(block.shape, block.dtype) for block in blocks]
    held.append(pltpu.SemaphoreType.DMA((3 * (NEAR_DEV // NEAR_CHUNK),)))
    return pl.pallas_call(
        first_kernel if first else second_kernel,
        out_shape=(half, half),
        in_specs=[HBM] * 6 + [VMEM] + [HBM if first else VMEM] * 3,
        out_specs=(VMEM, VMEM),
        scratch_shapes=(held if first else [])
        + [
            pltpu.VMEM((TARGETS + 1, 2 * OBJ, LEAF), jnp.bfloat16),
            pltpu.VMEM((SOURCES, OBJ, LEAF), jnp.float32),
            pltpu.SMEM((NEAR_DEV,), jnp.int32),
            pltpu.SMEM((NEAR_DEV,), jnp.int32),
            pltpu.SMEM((FAR_DEV,), jnp.int32),
            pltpu.SMEM((FAR_DEV,), jnp.int32),
            pltpu.SMEM((1,), jnp.int32),
            pltpu.SMEM((1,), jnp.int32),
            pltpu.SemaphoreType.DMA((6,)),
        ],
        compiler_params=pltpu.CompilerParams(vmem_limit_bytes=24 * 1024 * 1024),
        cost_estimate=pl.CostEstimate(flops=170_000_000, bytes_accessed=12_000_000, transcendentals=0),
    )(*lists, field, *blocks)


def to_all(value, axes):
    size = lax.axis_size(axes)
    return lax.all_to_all(jnp.broadcast_to(value[None], (size,) + value.shape), axes, split_axis=0, concat_axis=0)


def scatter_sum(keep, send):
    other = lax.ppermute((send * SCALE).astype(jnp.float16), "core", [(0, 1), (1, 0)])
    pieces = (keep * SCALE + other.astype(jnp.float32)).astype(jnp.float16).reshape(-1, CL_DEV, OBJ, LEAF)
    moved = lax.all_to_all(pieces, ("gy", "gq"), split_axis=0, concat_axis=0)
    return jnp.sum(moved.astype(jnp.float32), axis=0) * (1.0 / SCALE)


def gather_targets(value, scale):
    moved = to_all((value * scale).astype(jnp.float16), PLANE)
    return moved.astype(jnp.float32).reshape(TARGETS, OBJ, LEAF) * (1.0 / scale)


def dot(first, second):
    return jnp.sum(first * second, axis=(0, 2))


def column(value):
    return value[None, :, None]


def finish(sums_ref, r_ref, u_ref, applied_ref, basis_ref, entries_ref, fails_ref):
    sums = sums_ref[...]
    rr, ru, uu, rw, uw, ww = (sums[i : i + 1] for i in range(6))
    beta_sq = rr + EPS
    beta = jnp.sqrt(beta_sq)
    h11 = ru / beta_sq
    left_1 = (uu - 2.0 * h11 * ru + h11 * h11 * rr) / beta_sq
    h21 = jnp.sqrt(left_1 + EPS)
    scale = 1.0 / (beta * h21)
    g11 = rr / beta_sq
    g12 = (ru - h11 * rr) / beta_sq / h21
    g22 = left_1 / (left_1 + EPS)
    h12 = (rw - h11 * ru) / beta_sq / h21
    h22 = (uw - h11 * uu - h11 * (rw - h11 * ru)) * scale * scale
    image_sq = (ww - 2.0 * h11 * uw + h11 * h11 * uu) * scale * scale
    left_2 = image_sq - h12 * h12 * (2.0 - g11) - h22 * h22 * (2.0 - g22) + 2.0 * h12 * h22 * g12
    h32 = jnp.sqrt(left_2 + EPS)
    entries_ref[...] = jnp.concatenate([beta, h11, h21, h12, h22, h32], axis=0)
    in_w = scale / h32
    in_u = -(h11 + h22) * in_w
    in_r = (h11 * h22 * scale - h12 / beta) / h32
    own = lax.broadcasted_iota(jnp.int32, (OBJ, OBJ), 0) == lax.broadcasted_iota(jnp.int32, (OBJ, OBJ), 1)

    def down(row):
        return jnp.sum(jnp.where(own, row, 0.0), axis=1, keepdims=True)

    in_w, in_u, in_r = down(in_w), down(in_u), down(in_r)
    for i in range(CL_DEV):
        lanes = pl.ds(i * LEAF, LEAF)
        w = 0.5 * u_ref[i] + applied_ref[i]
        basis_ref[:, lanes] = in_w * w + in_u * u_ref[i] + in_r * r_ref[:, lanes]
    rest_1 = left_1 * beta_sq
    rest_2 = left_2 * beta_sq * h21 * h21
    sound = (rest_1 >= RATIO * uu) & (rest_2 >= RATIO * ww) & (rest_1 >= FLOOR) & (rest_2 >= FLOOR)
    fails_ref[0] = jnp.sum(jnp.where(sound, 0.0, 1.0)).astype(jnp.int32)


def plainly(r0, indices, blocks):
    r = jnp.swapaxes(r0.reshape(OBJ, CL_DEV, LEAF), 0, 1)
    nt, ns, nc, ft, fs, fc = indices
    near, left, right = blocks[0], jnp.swapaxes(blocks[1], 1, 2), jnp.swapaxes(blocks[2], 1, 2)
    near_alive = (jnp.arange(NEAR_DEV, dtype=jnp.int32) < nc[0]).astype(jnp.float32)
    far_alive = (jnp.arange(FAR_DEV, dtype=jnp.int32) < fc[0]).astype(jnp.float32)

    def total(first, second):
        plane = jnp.sum(to_all(dot(first, second)[None], PLANE), axis=0)
        return jnp.sum(to_all(plane, "gy"), axis=0)[0]

    def apply(vector):
        gathered = to_all(vector, PLANE).reshape(TARGETS, OBJ, LEAF).astype(jnp.bfloat16)
        partial = jnp.zeros((SOURCES, OBJ, LEAF), jnp.float32)
        picked = gathered[target_row(nt)]
        parts = jnp.einsum("bol,bls->bos", picked, near, preferred_element_type=jnp.float32)
        partial = partial.at[ns & (SOURCES - 1)].add(parts * near_alive[:, None, None])
        picked = gathered[target_row(ft)]
        reduced = jnp.einsum("bol,brl->bor", picked, left, preferred_element_type=jnp.float32).astype(jnp.bfloat16)
        parts = jnp.einsum("bor,brs->bos", reduced, right, preferred_element_type=jnp.float32)
        partial = partial.at[fs & (SOURCES - 1)].add(parts * far_alive[:, None, None])
        pieces = partial.reshape(-1, CL_DEV, OBJ, LEAF)
        moved = lax.all_to_all(pieces, ("gy", "gq", "core"), split_axis=0, concat_axis=0)
        return 0.5 * vector + jnp.sum(moved, axis=0)

    length = jnp.sqrt(total(r, r) + EPS)
    basis = [r / column(length)]
    entries = [length]
    for _ in range(2):
        image = apply(basis[-1])
        coeffs = [total(member, image) for member in basis]
        remainder = image
        for member, coeff in zip(basis, coeffs):
            remainder = remainder - column(coeff) * member
        length = jnp.sqrt(total(remainder, remainder) + EPS)
        basis.append(remainder / column(length))
        entries += coeffs + [length]
    return jnp.swapaxes(basis[-1], 0, 1).reshape(OBJ, CL_DEV * LEAF), jnp.stack(entries)


def on_device(r0, near_tiles, nt, ns, nc, far_left, far_right, ft, fs, fc):
    indices = (nt, ns, nc, ft, fs, fc)
    blocks = (near_tiles, jnp.swapaxes(far_left, 1, 2), jnp.swapaxes(far_right, 1, 2))
    r = jnp.swapaxes(r0.reshape(OBJ, CL_DEV, LEAF), 0, 1)

    lists = (nt, ns, ft, fs, nc, fc)
    u = 0.5 * r + scatter_sum(*product(lists, gather_targets(r, SCALE_R), blocks, True))
    applied = scatter_sum(*product(lists, gather_targets(u, SCALE), blocks, False))
    w = 0.5 * u + applied
    dots = [dot(r, r), dot(r, u), dot(u, u), dot(r, w), dot(u, w), dot(w, w)]
    local = jnp.concatenate(dots + [jnp.zeros((LEAF - len(dots) * OBJ,), jnp.float32)])[None]
    chip = local + lax.ppermute(local, "core", [(0, 1), (1, 0)])
    sums = jnp.sum(to_all(chip, ("gx", "gy", "gq")), axis=0)[0]
    sums = jnp.stack([sums[i * OBJ : (i + 1) * OBJ] for i in range(len(dots))])
    basis_3, entries, fails = pl.pallas_call(
        finish,
        out_shape=(
            jax.ShapeDtypeStruct((OBJ, CL_DEV * LEAF), jnp.float32),
            jax.ShapeDtypeStruct((6, OBJ), jnp.float32),
            jax.ShapeDtypeStruct((1,), jnp.int32),
        ),
        in_specs=[VMEM] * 4,
        out_specs=(VMEM, VMEM, SMEM),
        compiler_params=pltpu.CompilerParams(vmem_limit_bytes=2 * 1024 * 1024),
    )(sums, r0, u, applied)
    basis_3, entries = lax.switch(
        fails[0], (lambda: (basis_3, entries), lambda: plainly(r0, indices, (near_tiles, far_left, far_right)))
    )
    return basis_3, entries.T


def solution(mesh):
    fine = Mesh(mesh.devices.reshape(4, 8, 4, 2), ALL)
    spread = P(ALL)
    return jax.shard_map(
        on_device,
        mesh=fine,
        in_specs=(P(None, ALL),) + (spread,) * 9,
        out_specs=(P(None, ALL), P()),
        check_vma=False,
    )
```

```python
import jax
import jax.numpy as jnp
from jax import lax
from jax.experimental import pallas as pl
from jax.experimental.pallas import tpu as pltpu
from jax.sharding import Mesh
from jax.sharding import PartitionSpec as P

OBJ = 16
LEAF = 128
RANK = 64
CL_DEV = 2
NEAR_DEV = 128
FAR_DEV = 192
EPS = 1e-06

ALL = ("gx", "gy", "gq", "core")
PLANE = ("gx", "gq", "core")
TARGETS = 64
SOURCES = 128
NEAR_STEP = NEAR_CHUNK = 32
FAR_STEP = FAR_CHUNK = 48

SCALE_R = 2.0**15
SCALE = 2.0**4
RATIO = 1.0 / 1024.0
FLOOR = 1e-5

SMEM = pl.BlockSpec(memory_space=pltpu.SMEM)
VMEM = pl.BlockSpec(memory_space=pltpu.VMEM)
HBM = pl.BlockSpec(memory_space=pltpu.HBM)


def target_row(cluster):
    return (cluster >> 7) * 16 + (cluster & 15)


def start_blocks(near, left, right, near_v, left_v, right_v, sems):
    copies = []
    for i in range(NEAR_DEV // NEAR_CHUNK):
        near_part = pl.ds(i * NEAR_CHUNK, NEAR_CHUNK)
        far_part = pl.ds(i * FAR_CHUNK, FAR_CHUNK)
        for source, held, part in ((left, left_v, far_part), (near, near_v, near_part), (right, right_v, far_part)):
            copies.append(pltpu.make_async_copy(source.at[part], held.at[part], sems.at[len(copies)]))
    for copy in copies[:6]:
        copy.start()
    return copies


def two_terms(value):
    high = value.astype(jnp.bfloat16)
    return high, (value - high.astype(jnp.float32)).astype(jnp.bfloat16)


def first_kernel(*refs):
    *indices, field, near, left, right, keep, send, near_v, left_v, right_v, sems = refs[:16]
    multiply(*indices, field, near_v, left_v, right_v, keep, send, *refs[16:], blocks_in=(near, left, right, sems))


def second_kernel(*refs):
    multiply(*refs)


def multiply(
    nt, ns, ft, fs, nc, fc, field, near_v, left_v, right_v, keep, send,
    x, acc, nt_s, ns_s, ft_s, fs_s, nc_s, fc_s, index_sems, blocks_in=None,
):
    fetches = [
        pltpu.make_async_copy(source, held, index_sems.at[i])
        for i, (source, held) in enumerate(
            ((nt, nt_s), (ns, ns_s), (ft, ft_s), (fs, fs_s), (nc, nc_s), (fc, fc_s))
        )
    ]
    for fetch in fetches:
        fetch.start()
    if blocks_in:
        near, left, right, sems = blocks_in
        copies = start_blocks(near, left, right, near_v, left_v, right_v, sems)
    high, low = two_terms(field[...])
    x[:TARGETS, :OBJ] = high
    x[:TARGETS, OBJ:] = low
    x[TARGETS] = jnp.zeros((2 * OBJ, LEAF), jnp.bfloat16)
    acc[...] = jnp.zeros_like(acc)
    own_half = lax.broadcasted_iota(jnp.int32, (2 * OBJ, LEAF), 0) // OBJ == (
        lax.broadcasted_iota(jnp.int32, (2 * OBJ, LEAF), 1) // RANK
    )

    for fetch in fetches:
        fetch.wait()
    near_live = nc_s[0]
    far_live = fc_s[0]

    def rows(targets, live, slot, count):
        picked = [
            x[jnp.where(slot + i < live, target_row(targets[slot + i]), TARGETS)] for i in range(count)
        ]
        return jnp.concatenate(picked, axis=0)

    def add(parts, sources, slot):
        for i, part in enumerate(parts):
            acc[sources[slot + i] & (SOURCES - 1)] += part

    def step(index):
        near_first = index * NEAR_STEP
        far_first = index * FAR_STEP
        reduced = []
        for i in range(0, FAR_STEP, 4):
            slot = far_first + i
            lefts = left_v[pl.ds(slot, 4)].reshape(4 * RANK, LEAF)
            both = lax.dot_general(
                rows(ft_s, far_live, slot, 4), lefts, (((1,), (1,)), ((), ())), preferred_element_type=jnp.float32
            )
            for half in (both[: 4 * OBJ, :LEAF], both[4 * OBJ :, LEAF:]):
                pair = [half[j : j + OBJ] + half[j + OBJ : j + 2 * OBJ] for j in (0, 2 * OBJ)]
                reduced += two_terms(jnp.where(own_half, jnp.concatenate(pair, axis=0), 0.0))
        near_parts = []
        for i in range(0, NEAR_STEP, 2):
            slot = near_first + i
            pair = jnp.concatenate([near_v[slot], near_v[slot + 1]], axis=1)
            both = jnp.dot(rows(nt_s, near_live, slot, 2), pair, preferred_element_type=jnp.float32)
            near_parts.append(both[:OBJ, :LEAF] + both[OBJ : 2 * OBJ, :LEAF])
            near_parts.append(both[2 * OBJ : 3 * OBJ, LEAF:] + both[3 * OBJ :, LEAF:])
        add(near_parts, ns_s, near_first)
        far_parts = []
        for i in range(0, FAR_STEP, 4):
            slot = far_first + i
            rights = jnp.concatenate(
                [
                    right_v[pl.ds(slot, 2)].reshape(2 * RANK, LEAF),
                    right_v[pl.ds(slot + 2, 2)].reshape(2 * RANK, LEAF),
                ],
                axis=1,
            )
            both = jnp.dot(
                jnp.concatenate(reduced[i : i + 4], axis=0), rights, preferred_element_type=jnp.float32
            )
            for half in (both[: 4 * OBJ, :LEAF], both[4 * OBJ :, LEAF:]):
                far_parts += [half[j : j + OBJ] + half[j + 2 * OBJ : j + 3 * OBJ] for j in (0, OBJ)]
        add(far_parts, fs_s, far_first)

    steps = jnp.maximum((near_live + NEAR_STEP - 1) // NEAR_STEP, (far_live + FAR_STEP - 1) // FAR_STEP)

    def body(index, carry):
        step(index)
        return carry

    if blocks_in:
        for chunk in range(NEAR_DEV // NEAR_CHUNK):
            for copy in copies[3 * chunk : 3 * chunk + 3]:
                copy.wait()
            for copy in copies[3 * chunk + 6 : 3 * chunk + 9]:
                copy.start()
            lax.fori_loop(chunk, jnp.clip(steps, chunk, chunk + 1), body, 0)
    else:
        lax.fori_loop(0, steps, body, 0)
    core = lax.axis_index("core")
    by_core = acc.reshape(SOURCES // 4, 4, OBJ, LEAF)
    keep[...] = by_core[:, pl.ds(2 * core, 2)].reshape(keep.shape)
    send[...] = by_core[:, pl.ds(2 - 2 * core, 2)].reshape(send.shape)


def product(lists, field, blocks, first):
    half = jax.ShapeDtypeStruct((SOURCES // 2, OBJ, LEAF), jnp.float32)
    held = [pltpu.VMEM(block.shape, block.dtype) for block in blocks]
    held.append(pltpu.SemaphoreType.DMA((3 * (NEAR_DEV // NEAR_CHUNK),)))
    return pl.pallas_call(
        first_kernel if first else second_kernel,
        out_shape=(half, half),
        in_specs=[HBM] * 6 + [VMEM] + [HBM if first else VMEM] * 3,
        out_specs=(VMEM, VMEM),
        scratch_shapes=(held if first else [])
        + [
            pltpu.VMEM((TARGETS + 1, 2 * OBJ, LEAF), jnp.bfloat16),
            pltpu.VMEM((SOURCES, OBJ, LEAF), jnp.float32),
            pltpu.SMEM((NEAR_DEV,), jnp.int32),
            pltpu.SMEM((NEAR_DEV,), jnp.int32),
            pltpu.SMEM((FAR_DEV,), jnp.int32),
            pltpu.SMEM((FAR_DEV,), jnp.int32),
            pltpu.SMEM((1,), jnp.int32),
            pltpu.SMEM((1,), jnp.int32),
            pltpu.SemaphoreType.DMA((6,)),
        ],
        compiler_params=pltpu.CompilerParams(vmem_limit_bytes=24 * 1024 * 1024),
        cost_estimate=pl.CostEstimate(flops=170_000_000, bytes_accessed=12_000_000, transcendentals=0),
    )(*lists, field, *blocks)


def to_all(value, axes):
    size = lax.axis_size(axes)
    return lax.all_to_all(jnp.broadcast_to(value[None], (size,) + value.shape), axes, split_axis=0, concat_axis=0)


def scatter_sum(keep, send):
    other = lax.ppermute((send * SCALE).astype(jnp.float16), "core", [(0, 1), (1, 0)])
    pieces = (keep * SCALE + other.astype(jnp.float32)).astype(jnp.float16).reshape(-1, CL_DEV, OBJ, LEAF)
    moved = lax.all_to_all(pieces, ("gy", "gq"), split_axis=0, concat_axis=0)
    return jnp.sum(moved.astype(jnp.float32), axis=0)


def gather_targets(value, scale):
    moved = to_all((value * scale).astype(jnp.float16), PLANE)
    return moved.astype(jnp.float32).reshape(TARGETS, OBJ, LEAF) * (1.0 / scale)


def dot(first, second):
    return jnp.sum(first * second, axis=(0, 2))


def column(value):
    return value[None, :, None]


def finish(sums_ref, r_ref, u_ref, applied_ref, basis_ref, entries_ref, fails_ref):
    sums = sums_ref[...]
    rr, ru, uu, rw, uw, ww = (sums[i : i + 1] for i in range(6))
    beta_sq = rr + EPS
    beta = jnp.sqrt(beta_sq)
    h11 = ru / beta_sq
    left_1 = (uu - 2.0 * h11 * ru + h11 * h11 * rr) / beta_sq
    h21 = jnp.sqrt(left_1 + EPS)
    scale = 1.0 / (beta * h21)
    g11 = rr / beta_sq
    g12 = (ru - h11 * rr) / beta_sq / h21
    g22 = left_1 / (left_1 + EPS)
    h12 = (rw - h11 * ru) / beta_sq / h21
    h22 = (uw - h11 * uu - h11 * (rw - h11 * ru)) * scale * scale
    image_sq = (ww - 2.0 * h11 * uw + h11 * h11 * uu) * scale * scale
    left_2 = image_sq - h12 * h12 * (2.0 - g11) - h22 * h22 * (2.0 - g22) + 2.0 * h12 * h22 * g12
    h32 = jnp.sqrt(left_2 + EPS)
    entries_ref[...] = jnp.concatenate([beta, h11, h21, h12, h22, h32], axis=0)
    in_w = scale / h32
    in_u = -(h11 + h22) * in_w
    in_r = (h11 * h22 * scale - h12 / beta) / h32
    own = lax.broadcasted_iota(jnp.int32, (OBJ, OBJ), 0) == lax.broadcasted_iota(jnp.int32, (OBJ, OBJ), 1)

    def down(row):
        return jnp.sum(jnp.where(own, row, 0.0), axis=1, keepdims=True)

    in_w, in_u, in_r = down(in_w), down(in_u), down(in_r)
    for i in range(CL_DEV):
        lanes = pl.ds(i * LEAF, LEAF)
        w = 0.5 * u_ref[i] + applied_ref[i] * (1.0 / SCALE)
        basis_ref[:, lanes] = in_w * w + in_u * u_ref[i] + in_r * r_ref[:, lanes]
    rest_1 = left_1 * beta_sq
    rest_2 = left_2 * beta_sq * h21 * h21
    sound = (rest_1 >= RATIO * uu) & (rest_2 >= RATIO * ww) & (rest_1 >= FLOOR) & (rest_2 >= FLOOR)
    fails_ref[0] = jnp.sum(jnp.where(sound, 0.0, 1.0)).astype(jnp.int32)


def plainly(r0, indices, blocks):
    r = jnp.swapaxes(r0.reshape(OBJ, CL_DEV, LEAF), 0, 1)
    nt, ns, nc, ft, fs, fc = indices
    near, left, right = blocks[0], jnp.swapaxes(blocks[1], 1, 2), jnp.swapaxes(blocks[2], 1, 2)
    near_alive = (jnp.arange(NEAR_DEV, dtype=jnp.int32) < nc[0]).astype(jnp.float32)
    far_alive = (jnp.arange(FAR_DEV, dtype=jnp.int32) < fc[0]).astype(jnp.float32)

    def total(first, second):
        plane = jnp.sum(to_all(dot(first, second)[None], PLANE), axis=0)
        return jnp.sum(to_all(plane, "gy"), axis=0)[0]

    def apply(vector):
        gathered = to_all(vector, PLANE).reshape(TARGETS, OBJ, LEAF).astype(jnp.bfloat16)
        partial = jnp.zeros((SOURCES, OBJ, LEAF), jnp.float32)
        picked = gathered[target_row(nt)]
        parts = jnp.einsum("bol,bls->bos", picked, near, preferred_element_type=jnp.float32)
        partial = partial.at[ns & (SOURCES - 1)].add(parts * near_alive[:, None, None])
        picked = gathered[target_row(ft)]
        reduced = jnp.einsum("bol,brl->bor", picked, left, preferred_element_type=jnp.float32).astype(jnp.bfloat16)
        parts = jnp.einsum("bor,brs->bos", reduced, right, preferred_element_type=jnp.float32)
        partial = partial.at[fs & (SOURCES - 1)].add(parts * far_alive[:, None, None])
        pieces = partial.reshape(-1, CL_DEV, OBJ, LEAF)
        moved = lax.all_to_all(pieces, ("gy", "gq", "core"), split_axis=0, concat_axis=0)
        return 0.5 * vector + jnp.sum(moved, axis=0)

    length = jnp.sqrt(total(r, r) + EPS)
    basis = [r / column(length)]
    entries = [length]
    for _ in range(2):
        image = apply(basis[-1])
        coeffs = [total(member, image) for member in basis]
        remainder = image
        for member, coeff in zip(basis, coeffs):
            remainder = remainder - column(coeff) * member
        length = jnp.sqrt(total(remainder, remainder) + EPS)
        basis.append(remainder / column(length))
        entries += coeffs + [length]
    return jnp.swapaxes(basis[-1], 0, 1).reshape(OBJ, CL_DEV * LEAF), jnp.stack(entries)


def on_device(r0, near_tiles, nt, ns, nc, far_left, far_right, ft, fs, fc):
    indices = (nt, ns, nc, ft, fs, fc)
    blocks = (near_tiles, jnp.swapaxes(far_left, 1, 2), jnp.swapaxes(far_right, 1, 2))
    r = jnp.swapaxes(r0.reshape(OBJ, CL_DEV, LEAF), 0, 1)

    lists = (nt, ns, ft, fs, nc, fc)
    applied = scatter_sum(*product(lists, gather_targets(r, SCALE_R), blocks, True))
    u = 0.5 * r + applied * (1.0 / SCALE)
    applied = scatter_sum(*product(lists, gather_targets(u, SCALE), blocks, False))
    w = 0.5 * u + applied * (1.0 / SCALE)
    dots = [dot(r, r), dot(r, u), dot(u, u), dot(r, w), dot(u, w), dot(w, w)]
    local = jnp.concatenate(dots + [jnp.zeros((LEAF - len(dots) * OBJ,), jnp.float32)])[None]
    chip = local + lax.ppermute(local, "core", [(0, 1), (1, 0)])
    sums = jnp.sum(to_all(chip, ("gx", "gy", "gq")), axis=0)[0]
    sums = jnp.stack([sums[i * OBJ : (i + 1) * OBJ] for i in range(len(dots))])
    basis_3, entries, fails = pl.pallas_call(
        finish,
        out_shape=(
            jax.ShapeDtypeStruct((OBJ, CL_DEV * LEAF), jnp.float32),
            jax.ShapeDtypeStruct((6, OBJ), jnp.float32),
            jax.ShapeDtypeStruct((1,), jnp.int32),
        ),
        in_specs=[VMEM] * 4,
        out_specs=(VMEM, VMEM, SMEM),
        compiler_params=pltpu.CompilerParams(vmem_limit_bytes=2 * 1024 * 1024),
    )(sums, r0, u, applied)
    basis_3, entries = lax.switch(
        fails[0], (lambda: (basis_3, entries), lambda: plainly(r0, indices, (near_tiles, far_left, far_right)))
    )
    return basis_3, entries.T


def solution(mesh):
    fine = Mesh(mesh.devices.reshape(4, 8, 4, 2), ALL)
    spread = P(ALL)
    return jax.shard_map(
        on_device,
        mesh=fine,
        in_specs=(P(None, ALL),) + (spread,) * 9,
        out_specs=(P(None, ALL), P()),
        check_vma=False,
    )
```

```python
import jax
import jax.numpy as jnp
from jax import lax
from jax.experimental import pallas as pl
from jax.experimental.pallas import tpu as pltpu
from jax.sharding import Mesh
from jax.sharding import PartitionSpec as P

OBJ = 16
LEAF = 128
RANK = 64
CL_DEV = 2
NEAR_DEV = 128
FAR_DEV = 192
EPS = 1e-06

ALL = ("gx", "gy", "gq", "core")
PLANE = ("gx", "gq", "core")
TARGETS = 64
SOURCES = 128
NEAR_STEP = 32
FAR_STEP = 48
STEPS = 4
PARTS = 2

SCALE_R = 2.0**15
SCALE = 2.0**4
RATIO = 1.0 / 1024.0
FLOOR = 1e-5

SMEM = pl.BlockSpec(memory_space=pltpu.SMEM)
VMEM = pl.BlockSpec(memory_space=pltpu.VMEM)
HBM = pl.BlockSpec(memory_space=pltpu.HBM)


def target_row(cluster):
    return (cluster >> 7) * 16 + (cluster & 15)


def start_blocks(near, left, right, near_v, left_v, right_v, sems):
    copies = []
    for i in range(STEPS * PARTS):
        near_part = pl.ds(i * (NEAR_STEP // PARTS), NEAR_STEP // PARTS)
        far_part = pl.ds(i * (FAR_STEP // PARTS), FAR_STEP // PARTS)
        for source, held, part in ((left, left_v, far_part), (near, near_v, near_part), (right, right_v, far_part)):
            copies.append(pltpu.make_async_copy(source.at[part], held.at[part], sems.at[len(copies)]))
    for copy in copies:
        copy.start()
    return copies


def two_terms(value):
    high = value.astype(jnp.bfloat16)
    return high, (value - high.astype(jnp.float32)).astype(jnp.bfloat16)


def first_kernel(*refs):
    *indices, field, near, left, right, keep, send, near_v, left_v, right_v, sems = refs[:16]
    multiply(*indices, field, near_v, left_v, right_v, keep, send, *refs[16:], blocks_in=(near, left, right, sems))


def second_kernel(*refs):
    multiply(*refs)


def multiply(
    nt, ns, ft, fs, nc, fc, field, near_v, left_v, right_v, keep, send,
    x, acc, nt_s, ns_s, ft_s, fs_s, nc_s, fc_s, index_sems, blocks_in=None,
):
    fetches = [
        pltpu.make_async_copy(source, held, index_sems.at[i])
        for i, (source, held) in enumerate(
            ((nt, nt_s), (ns, ns_s), (ft, ft_s), (fs, fs_s), (nc, nc_s), (fc, fc_s))
        )
    ]
    for fetch in fetches:
        fetch.start()
    if blocks_in:
        near, left, right, sems = blocks_in
        copies = start_blocks(near, left, right, near_v, left_v, right_v, sems)
    high, low = two_terms(field[...])
    x[:TARGETS, :OBJ] = high
    x[:TARGETS, OBJ:] = low
    x[TARGETS] = jnp.zeros((2 * OBJ, LEAF), jnp.bfloat16)
    acc[...] = jnp.zeros_like(acc)
    own_half = lax.broadcasted_iota(jnp.int32, (2 * OBJ, LEAF), 0) // OBJ == (
        lax.broadcasted_iota(jnp.int32, (2 * OBJ, LEAF), 1) // RANK
    )

    for fetch in fetches:
        fetch.wait()
    near_live = nc_s[0]
    far_live = fc_s[0]

    def rows(targets, live, slot, count):
        picked = [
            x[jnp.where(slot + i < live, target_row(targets[slot + i]), TARGETS)] for i in range(count)
        ]
        return jnp.concatenate(picked, axis=0)

    def add(parts, sources, slot):
        for i, part in enumerate(parts):
            acc[sources[slot + i] & (SOURCES - 1)] += part

    def step(index):
        near_first = index * NEAR_STEP
        far_first = index * FAR_STEP
        reduced = []
        for i in range(0, FAR_STEP, 4):
            slot = far_first + i
            lefts = left_v[pl.ds(slot, 4)].reshape(4 * RANK, LEAF)
            both = lax.dot_general(
                rows(ft_s, far_live, slot, 4), lefts, (((1,), (1,)), ((), ())), preferred_element_type=jnp.float32
            )
            for half in (both[: 4 * OBJ, :LEAF], both[4 * OBJ :, LEAF:]):
                pair = [half[j : j + OBJ] + half[j + OBJ : j + 2 * OBJ] for j in (0, 2 * OBJ)]
                reduced += two_terms(jnp.where(own_half, jnp.concatenate(pair, axis=0), 0.0))
        near_parts = []
        for i in range(0, NEAR_STEP, 2):
            slot = near_first + i
            pair = jnp.concatenate([near_v[slot], near_v[slot + 1]], axis=1)
            both = jnp.dot(rows(nt_s, near_live, slot, 2), pair, preferred_element_type=jnp.float32)
            near_parts.append(both[:OBJ, :LEAF] + both[OBJ : 2 * OBJ, :LEAF])
            near_parts.append(both[2 * OBJ : 3 * OBJ, LEAF:] + both[3 * OBJ :, LEAF:])
        add(near_parts, ns_s, near_first)
        far_parts = []
        for i in range(0, FAR_STEP, 4):
            slot = far_first + i
            rights = jnp.concatenate(
                [
                    right_v[pl.ds(slot, 2)].reshape(2 * RANK, LEAF),
                    right_v[pl.ds(slot + 2, 2)].reshape(2 * RANK, LEAF),
                ],
                axis=1,
            )
            both = jnp.dot(
                jnp.concatenate(reduced[i : i + 4], axis=0), rights, preferred_element_type=jnp.float32
            )
            for half in (both[: 4 * OBJ, :LEAF], both[4 * OBJ :, LEAF:]):
                far_parts += [half[j : j + OBJ] + half[j + 2 * OBJ : j + 3 * OBJ] for j in (0, OBJ)]
        add(far_parts, fs_s, far_first)

    steps = jnp.maximum((near_live + NEAR_STEP - 1) // NEAR_STEP, (far_live + FAR_STEP - 1) // FAR_STEP)

    def body(index, carry):
        step(index)
        return carry

    if blocks_in:
        for chunk in range(STEPS):
            for copy in copies[3 * PARTS * chunk : 3 * PARTS * (chunk + 1)]:
                copy.wait()
            lax.fori_loop(chunk, jnp.clip(steps, chunk, chunk + 1), body, 0)
    else:
        lax.fori_loop(0, steps, body, 0)
    core = lax.axis_index("core")
    by_core = acc.reshape(SOURCES // 4, 4, OBJ, LEAF)
    keep[...] = by_core[:, pl.ds(2 * core, 2)].reshape(keep.shape)
    send[...] = by_core[:, pl.ds(2 - 2 * core, 2)].reshape(send.shape)


def product(lists, field, blocks, first):
    half = jax.ShapeDtypeStruct((SOURCES // 2, OBJ, LEAF), jnp.float32)
    held = [pltpu.VMEM(block.shape, block.dtype) for block in blocks]
    held.append(pltpu.SemaphoreType.DMA((3 * STEPS * PARTS,)))
    return pl.pallas_call(
        first_kernel if first else second_kernel,
        out_shape=(half, half),
        in_specs=[HBM] * 6 + [VMEM] + [HBM if first else VMEM] * 3,
        out_specs=(VMEM, VMEM),
        scratch_shapes=(held if first else [])
        + [
            pltpu.VMEM((TARGETS + 1, 2 * OBJ, LEAF), jnp.bfloat16),
            pltpu.VMEM((SOURCES, OBJ, LEAF), jnp.float32),
            pltpu.SMEM((NEAR_DEV,), jnp.int32),
            pltpu.SMEM((NEAR_DEV,), jnp.int32),
            pltpu.SMEM((FAR_DEV,), jnp.int32),
            pltpu.SMEM((FAR_DEV,), jnp.int32),
            pltpu.SMEM((1,), jnp.int32),
            pltpu.SMEM((1,), jnp.int32),
            pltpu.SemaphoreType.DMA((6,)),
        ],
        compiler_params=pltpu.CompilerParams(vmem_limit_bytes=24 * 1024 * 1024),
        cost_estimate=pl.CostEstimate(flops=170_000_000, bytes_accessed=12_000_000, transcendentals=0),
    )(*lists, field, *blocks)


def to_all(value, axes):
    size = lax.axis_size(axes)
    return lax.all_to_all(jnp.broadcast_to(value[None], (size,) + value.shape), axes, split_axis=0, concat_axis=0)


def scatter_sum(keep, send):
    other = lax.ppermute((send * SCALE).astype(jnp.float16), "core", [(0, 1), (1, 0)])
    pieces = (keep * SCALE + other.astype(jnp.float32)).astype(jnp.float16).reshape(-1, CL_DEV, OBJ, LEAF)
    moved = lax.all_to_all(pieces, ("gy", "gq"), split_axis=0, concat_axis=0)
    return jnp.sum(moved.astype(jnp.float32), axis=0)


def gather_targets(value, scale):
    moved = to_all((value * scale).astype(jnp.float16), PLANE)
    return moved.astype(jnp.float32).reshape(TARGETS, OBJ, LEAF) * (1.0 / scale)


def dot(first, second):
    return jnp.sum(first * second, axis=(0, 2))


def column(value):
    return value[None, :, None]


def finish(sums_ref, r_ref, u_ref, applied_ref, basis_ref, entries_ref, fails_ref):
    sums = sums_ref[...]
    rr, ru, uu, rw, uw, ww = (sums[i : i + 1] for i in range(6))
    beta_sq = rr + EPS
    beta = jnp.sqrt(beta_sq)
    h11 = ru / beta_sq
    left_1 = (uu - 2.0 * h11 * ru + h11 * h11 * rr) / beta_sq
    h21 = jnp.sqrt(left_1 + EPS)
    scale = 1.0 / (beta * h21)
    g11 = rr / beta_sq
    g12 = (ru - h11 * rr) / beta_sq / h21
    g22 = left_1 / (left_1 + EPS)
    h12 = (rw - h11 * ru) / beta_sq / h21
    h22 = (uw - h11 * uu - h11 * (rw - h11 * ru)) * scale * scale
    image_sq = (ww - 2.0 * h11 * uw + h11 * h11 * uu) * scale * scale
    left_2 = image_sq - h12 * h12 * (2.0 - g11) - h22 * h22 * (2.0 - g22) + 2.0 * h12 * h22 * g12
    h32 = jnp.sqrt(left_2 + EPS)
    entries_ref[...] = jnp.concatenate([beta, h11, h21, h12, h22, h32], axis=0)
    in_w = scale / h32
    in_u = -(h11 + h22) * in_w
    in_r = (h11 * h22 * scale - h12 / beta) / h32
    own = lax.broadcasted_iota(jnp.int32, (OBJ, OBJ), 0) == lax.broadcasted_iota(jnp.int32, (OBJ, OBJ), 1)

    def down(row):
        return jnp.sum(jnp.where(own, row, 0.0), axis=1, keepdims=True)

    in_w, in_u, in_r = down(in_w), down(in_u), down(in_r)
    for i in range(CL_DEV):
        lanes = pl.ds(i * LEAF, LEAF)
        w = 0.5 * u_ref[i] + applied_ref[i] * (1.0 / SCALE)
        basis_ref[:, lanes] = in_w * w + in_u * u_ref[i] + in_r * r_ref[:, lanes]
    rest_1 = left_1 * beta_sq
    rest_2 = left_2 * beta_sq * h21 * h21
    sound = (rest_1 >= RATIO * uu) & (rest_2 >= RATIO * ww) & (rest_1 >= FLOOR) & (rest_2 >= FLOOR)
    fails_ref[0] = jnp.sum(jnp.where(sound, 0.0, 1.0)).astype(jnp.int32)


def plainly(r0, indices, blocks):
    r = jnp.swapaxes(r0.reshape(OBJ, CL_DEV, LEAF), 0, 1)
    nt, ns, nc, ft, fs, fc = indices
    near, left, right = blocks[0], jnp.swapaxes(blocks[1], 1, 2), jnp.swapaxes(blocks[2], 1, 2)
    near_alive = (jnp.arange(NEAR_DEV, dtype=jnp.int32) < nc[0]).astype(jnp.float32)
    far_alive = (jnp.arange(FAR_DEV, dtype=jnp.int32) < fc[0]).astype(jnp.float32)

    def total(first, second):
        plane = jnp.sum(to_all(dot(first, second)[None], PLANE), axis=0)
        return jnp.sum(to_all(plane, "gy"), axis=0)[0]

    def apply(vector):
        gathered = to_all(vector, PLANE).reshape(TARGETS, OBJ, LEAF).astype(jnp.bfloat16)
        partial = jnp.zeros((SOURCES, OBJ, LEAF), jnp.float32)
        picked = gathered[target_row(nt)]
        parts = jnp.einsum("bol,bls->bos", picked, near, preferred_element_type=jnp.float32)
        partial = partial.at[ns & (SOURCES - 1)].add(parts * near_alive[:, None, None])
        picked = gathered[target_row(ft)]
        reduced = jnp.einsum("bol,brl->bor", picked, left, preferred_element_type=jnp.float32).astype(jnp.bfloat16)
        parts = jnp.einsum("bor,brs->bos", reduced, right, preferred_element_type=jnp.float32)
        partial = partial.at[fs & (SOURCES - 1)].add(parts * far_alive[:, None, None])
        pieces = partial.reshape(-1, CL_DEV, OBJ, LEAF)
        moved = lax.all_to_all(pieces, ("gy", "gq", "core"), split_axis=0, concat_axis=0)
        return 0.5 * vector + jnp.sum(moved, axis=0)

    length = jnp.sqrt(total(r, r) + EPS)
    basis = [r / column(length)]
    entries = [length]
    for _ in range(2):
        image = apply(basis[-1])
        coeffs = [total(member, image) for member in basis]
        remainder = image
        for member, coeff in zip(basis, coeffs):
            remainder = remainder - column(coeff) * member
        length = jnp.sqrt(total(remainder, remainder) + EPS)
        basis.append(remainder / column(length))
        entries += coeffs + [length]
    return jnp.swapaxes(basis[-1], 0, 1).reshape(OBJ, CL_DEV * LEAF), jnp.stack(entries)


def on_device(r0, near_tiles, nt, ns, nc, far_left, far_right, ft, fs, fc):
    indices = (nt, ns, nc, ft, fs, fc)
    blocks = (near_tiles, jnp.swapaxes(far_left, 1, 2), jnp.swapaxes(far_right, 1, 2))
    r = jnp.swapaxes(r0.reshape(OBJ, CL_DEV, LEAF), 0, 1)

    lists = (nt, ns, ft, fs, nc, fc)
    applied = scatter_sum(*product(lists, gather_targets(r, SCALE_R), blocks, True))
    u = 0.5 * r + applied * (1.0 / SCALE)
    applied = scatter_sum(*product(lists, gather_targets(u, SCALE), blocks, False))
    w = 0.5 * u + applied * (1.0 / SCALE)
    dots = [dot(r, r), dot(r, u), dot(u, u), dot(r, w), dot(u, w), dot(w, w)]
    local = jnp.concatenate(dots + [jnp.zeros((LEAF - len(dots) * OBJ,), jnp.float32)])[None]
    chip = local + lax.ppermute(local, "core", [(0, 1), (1, 0)])
    sums = jnp.sum(to_all(chip, ("gx", "gy", "gq")), axis=0)[0]
    sums = jnp.stack([sums[i * OBJ : (i + 1) * OBJ] for i in range(len(dots))])
    basis_3, entries, fails = pl.pallas_call(
        finish,
        out_shape=(
            jax.ShapeDtypeStruct((OBJ, CL_DEV * LEAF), jnp.float32),
            jax.ShapeDtypeStruct((6, OBJ), jnp.float32),
            jax.ShapeDtypeStruct((1,), jnp.int32),
        ),
        in_specs=[VMEM] * 4,
        out_specs=(VMEM, VMEM, SMEM),
        compiler_params=pltpu.CompilerParams(vmem_limit_bytes=2 * 1024 * 1024),
    )(sums, r0, u, applied)
    def branch():
        plain = plainly(r0, indices, (near_tiles, far_left, far_right))
        return tuple(jnp.where(fails[0] > 0, new, old) for new, old in zip(plain, (basis_3, entries)))

    basis_3, entries = lax.switch(fails[0], (lambda: (basis_3, entries), branch))
    return basis_3, entries.T


def solution(mesh):
    fine = Mesh(mesh.devices.reshape(4, 8, 4, 2), ALL)
    spread = P(ALL)
    return jax.shard_map(
        on_device,
        mesh=fine,
        in_specs=(P(None, ALL),) + (spread,) * 9,
        out_specs=(P(None, ALL), P()),
        check_vma=False,
    )
```

```python
import jax
import jax.numpy as jnp
from jax import lax
from jax.experimental import pallas as pl
from jax.experimental.pallas import tpu as pltpu
from jax.sharding import Mesh
from jax.sharding import PartitionSpec as P

OBJ = 16
LEAF = 128
RANK = 64
CL_DEV = 2
NEAR_DEV = 128
FAR_DEV = 192
EPS = 1e-06

ALL = ("gx", "gy", "gq", "core")
PLANE = ("gx", "gq", "core")
TARGETS = 64
SOURCES = 128
NEAR_STEP = 32
FAR_STEP = 48
STEPS = 4
PARTS = 2

SCALE_R = 2.0**15
SCALE = 2.0**4
RATIO = 1.0 / 1024.0
FLOOR = 1e-5

SMEM = pl.BlockSpec(memory_space=pltpu.SMEM)
VMEM = pl.BlockSpec(memory_space=pltpu.VMEM)
HBM = pl.BlockSpec(memory_space=pltpu.HBM)


def target_row(cluster):
    return (cluster >> 7) * 16 + (cluster & 15)


def start_blocks(near, left, right, near_v, left_v, right_v, sems):
    copies = []
    for i in range(STEPS * PARTS):
        near_part = pl.ds(i * (NEAR_STEP // PARTS), NEAR_STEP // PARTS)
        far_part = pl.ds(i * (FAR_STEP // PARTS), FAR_STEP // PARTS)
        for source, held, part in ((left, left_v, far_part), (near, near_v, near_part), (right, right_v, far_part)):
            copies.append(pltpu.make_async_copy(source.at[part], held.at[part], sems.at[len(copies)]))
    for copy in copies:
        copy.start()
    return copies


def two_terms(value):
    high = value.astype(jnp.bfloat16)
    return high, (value - high.astype(jnp.float32)).astype(jnp.bfloat16)


def first_kernel(*refs):
    *indices, field, near, left, right, keep, send, near_v, left_v, right_v, sems = refs[:16]
    multiply(*indices, field, near_v, left_v, right_v, keep, send, *refs[16:], blocks_in=(near, left, right, sems))


def second_kernel(*refs):
    multiply(*refs)


def multiply(
    nt, ns, ft, fs, nc, fc, field, near_v, left_v, right_v, keep, send,
    x, acc, nt_s, ns_s, ft_s, fs_s, nc_s, fc_s, index_sems, blocks_in=None,
):
    fetches = [
        pltpu.make_async_copy(source, held, index_sems.at[i])
        for i, (source, held) in enumerate(
            ((nt, nt_s), (ns, ns_s), (ft, ft_s), (fs, fs_s), (nc, nc_s), (fc, fc_s))
        )
    ]
    for fetch in fetches:
        fetch.start()
    if blocks_in:
        near, left, right, sems = blocks_in
        copies = start_blocks(near, left, right, near_v, left_v, right_v, sems)
    high, low = two_terms(field[...])
    x[:TARGETS, :OBJ] = high
    x[:TARGETS, OBJ:] = low
    x[TARGETS] = jnp.zeros((2 * OBJ, LEAF), jnp.bfloat16)
    acc[...] = jnp.zeros_like(acc)
    own_half = lax.broadcasted_iota(jnp.int32, (2 * OBJ, LEAF), 0) // OBJ == (
        lax.broadcasted_iota(jnp.int32, (2 * OBJ, LEAF), 1) // RANK
    )

    for fetch in fetches:
        fetch.wait()
    near_live = nc_s[0]
    far_live = fc_s[0]

    def rows(targets, live, slot, count):
        picked = [
            x[jnp.where(slot + i < live, target_row(targets[slot + i]), TARGETS)] for i in range(count)
        ]
        return jnp.concatenate(picked, axis=0)

    def add(parts, sources, slot):
        for i, part in enumerate(parts):
            acc[sources[slot + i] & (SOURCES - 1)] += part

    def step(index):
        near_first = index * NEAR_STEP
        far_first = index * FAR_STEP
        reduced = []
        for i in range(0, FAR_STEP, 4):
            slot = far_first + i
            lefts = left_v[pl.ds(slot, 4)].reshape(4 * RANK, LEAF)
            both = lax.dot_general(
                rows(ft_s, far_live, slot, 4), lefts, (((1,), (1,)), ((), ())), preferred_element_type=jnp.float32
            )
            for half in (both[: 4 * OBJ, :LEAF], both[4 * OBJ :, LEAF:]):
                pair = [half[j : j + OBJ] + half[j + OBJ : j + 2 * OBJ] for j in (0, 2 * OBJ)]
                reduced += two_terms(jnp.where(own_half, jnp.concatenate(pair, axis=0), 0.0))
        near_parts = []
        for i in range(0, NEAR_STEP, 2):
            slot = near_first + i
            pair = jnp.concatenate([near_v[slot], near_v[slot + 1]], axis=1)
            both = jnp.dot(rows(nt_s, near_live, slot, 2), pair, preferred_element_type=jnp.float32)
            near_parts.append(both[:OBJ, :LEAF] + both[OBJ : 2 * OBJ, :LEAF])
            near_parts.append(both[2 * OBJ : 3 * OBJ, LEAF:] + both[3 * OBJ :, LEAF:])
        add(near_parts, ns_s, near_first)
        far_parts = []
        for i in range(0, FAR_STEP, 4):
            slot = far_first + i
            rights = jnp.concatenate(
                [
                    right_v[pl.ds(slot, 2)].reshape(2 * RANK, LEAF),
                    right_v[pl.ds(slot + 2, 2)].reshape(2 * RANK, LEAF),
                ],
                axis=1,
            )
            both = jnp.dot(
                jnp.concatenate(reduced[i : i + 4], axis=0), rights, preferred_element_type=jnp.float32
            )
            for half in (both[: 4 * OBJ, :LEAF], both[4 * OBJ :, LEAF:]):
                far_parts += [half[j : j + OBJ] + half[j + 2 * OBJ : j + 3 * OBJ] for j in (0, OBJ)]
        add(far_parts, fs_s, far_first)

    steps = jnp.maximum((near_live + NEAR_STEP - 1) // NEAR_STEP, (far_live + FAR_STEP - 1) // FAR_STEP)

    def body(index, carry):
        step(index)
        return carry

    if blocks_in:
        for chunk in range(STEPS):
            for copy in copies[3 * PARTS * chunk : 3 * PARTS * (chunk + 1)]:
                copy.wait()
            lax.fori_loop(chunk, jnp.clip(steps, chunk, chunk + 1), body, 0)
    else:
        lax.fori_loop(0, steps, body, 0)
    core = lax.axis_index("core")
    by_core = acc.reshape(8, 4, 4, OBJ, LEAF)
    for i in range(4):
        part = pl.ds(16 * i, 16)
        keep[part] = by_core[:, i, pl.ds(2 * core, 2)].reshape(16, OBJ, LEAF)
        send[part] = by_core[:, i, pl.ds(2 - 2 * core, 2)].reshape(16, OBJ, LEAF)


def product(lists, field, blocks, first):
    half = jax.ShapeDtypeStruct((SOURCES // 2, OBJ, LEAF), jnp.float32)
    held = [pltpu.VMEM(block.shape, block.dtype) for block in blocks]
    held.append(pltpu.SemaphoreType.DMA((3 * STEPS * PARTS,)))
    return pl.pallas_call(
        first_kernel if first else second_kernel,
        out_shape=(half, half),
        in_specs=[HBM] * 6 + [VMEM] + [HBM if first else VMEM] * 3,
        out_specs=(VMEM, VMEM),
        scratch_shapes=(held if first else [])
        + [
            pltpu.VMEM((TARGETS + 1, 2 * OBJ, LEAF), jnp.bfloat16),
            pltpu.VMEM((SOURCES, OBJ, LEAF), jnp.float32),
            pltpu.SMEM((NEAR_DEV,), jnp.int32),
            pltpu.SMEM((NEAR_DEV,), jnp.int32),
            pltpu.SMEM((FAR_DEV,), jnp.int32),
            pltpu.SMEM((FAR_DEV,), jnp.int32),
            pltpu.SMEM((1,), jnp.int32),
            pltpu.SMEM((1,), jnp.int32),
            pltpu.SemaphoreType.DMA((6,)),
        ],
        compiler_params=pltpu.CompilerParams(vmem_limit_bytes=24 * 1024 * 1024),
        cost_estimate=pl.CostEstimate(flops=170_000_000, bytes_accessed=12_000_000, transcendentals=0),
    )(*lists, field, *blocks)


def to_all(value, axes):
    size = lax.axis_size(axes)
    return lax.all_to_all(jnp.broadcast_to(value[None], (size,) + value.shape), axes, split_axis=0, concat_axis=0)


def scatter_sum(keep, send):
    other = lax.ppermute((send * SCALE).astype(jnp.float16), "core", [(0, 1), (1, 0)])
    pieces = (keep * SCALE + other.astype(jnp.float32)).astype(jnp.float16).reshape(-1, CL_DEV, OBJ, LEAF)
    moved = lax.all_to_all(pieces, ("gq", "gy"), split_axis=0, concat_axis=0)
    return jnp.sum(moved.astype(jnp.float32), axis=0)


def gather_targets(value, scale):
    moved = to_all((value * scale).astype(jnp.float16), PLANE)
    return moved.astype(jnp.float32).reshape(TARGETS, OBJ, LEAF) * (1.0 / scale)


def dot(first, second):
    return jnp.sum(first * second, axis=(0, 2))


def column(value):
    return value[None, :, None]


def finish(sums_ref, r_ref, u_ref, applied_ref, basis_ref, entries_ref, fails_ref):
    sums = sums_ref[...]
    rr, ru, uu, rw, uw, ww = (sums[i : i + 1] for i in range(6))
    beta_sq = rr + EPS
    beta = jnp.sqrt(beta_sq)
    h11 = ru / beta_sq
    left_1 = (uu - 2.0 * h11 * ru + h11 * h11 * rr) / beta_sq
    h21 = jnp.sqrt(left_1 + EPS)
    scale = 1.0 / (beta * h21)
    g11 = rr / beta_sq
    g12 = (ru - h11 * rr) / beta_sq / h21
    g22 = left_1 / (left_1 + EPS)
    h12 = (rw - h11 * ru) / beta_sq / h21
    h22 = (uw - h11 * uu - h11 * (rw - h11 * ru)) * scale * scale
    image_sq = (ww - 2.0 * h11 * uw + h11 * h11 * uu) * scale * scale
    left_2 = image_sq - h12 * h12 * (2.0 - g11) - h22 * h22 * (2.0 - g22) + 2.0 * h12 * h22 * g12
    h32 = jnp.sqrt(left_2 + EPS)
    entries_ref[...] = jnp.concatenate([beta, h11, h21, h12, h22, h32], axis=0)
    in_w = scale / h32
    in_u = -(h11 + h22) * in_w
    in_r = (h11 * h22 * scale - h12 / beta) / h32
    own = lax.broadcasted_iota(jnp.int32, (OBJ, OBJ), 0) == lax.broadcasted_iota(jnp.int32, (OBJ, OBJ), 1)

    def down(row):
        return jnp.sum(jnp.where(own, row, 0.0), axis=1, keepdims=True)

    in_w, in_u, in_r = down(in_w), down(in_u), down(in_r)
    for i in range(CL_DEV):
        lanes = pl.ds(i * LEAF, LEAF)
        w = 0.5 * u_ref[i] + applied_ref[i] * (1.0 / SCALE)
        basis_ref[:, lanes] = in_w * w + in_u * u_ref[i] + in_r * r_ref[:, lanes]
    rest_1 = left_1 * beta_sq
    rest_2 = left_2 * beta_sq * h21 * h21
    sound = (rest_1 >= RATIO * uu) & (rest_2 >= RATIO * ww) & (rest_1 >= FLOOR) & (rest_2 >= FLOOR)
    fails_ref[0] = jnp.sum(jnp.where(sound, 0.0, 1.0)).astype(jnp.int32)


def plainly(r0, indices, blocks):
    r = jnp.swapaxes(r0.reshape(OBJ, CL_DEV, LEAF), 0, 1)
    nt, ns, nc, ft, fs, fc = indices
    near, left, right = blocks[0], jnp.swapaxes(blocks[1], 1, 2), jnp.swapaxes(blocks[2], 1, 2)
    near_alive = (jnp.arange(NEAR_DEV, dtype=jnp.int32) < nc[0]).astype(jnp.float32)
    far_alive = (jnp.arange(FAR_DEV, dtype=jnp.int32) < fc[0]).astype(jnp.float32)

    def total(first, second):
        plane = jnp.sum(to_all(dot(first, second)[None], PLANE), axis=0)
        return jnp.sum(to_all(plane, "gy"), axis=0)[0]

    def apply(vector):
        gathered = to_all(vector, PLANE).reshape(TARGETS, OBJ, LEAF).astype(jnp.bfloat16)
        partial = jnp.zeros((SOURCES, OBJ, LEAF), jnp.float32)
        picked = gathered[target_row(nt)]
        parts = jnp.einsum("bol,bls->bos", picked, near, preferred_element_type=jnp.float32)
        partial = partial.at[ns & (SOURCES - 1)].add(parts * near_alive[:, None, None])
        picked = gathered[target_row(ft)]
        reduced = jnp.einsum("bol,brl->bor", picked, left, preferred_element_type=jnp.float32).astype(jnp.bfloat16)
        parts = jnp.einsum("bor,brs->bos", reduced, right, preferred_element_type=jnp.float32)
        partial = partial.at[fs & (SOURCES - 1)].add(parts * far_alive[:, None, None])
        pieces = partial.reshape(-1, CL_DEV, OBJ, LEAF)
        moved = lax.all_to_all(pieces, ("gy", "gq", "core"), split_axis=0, concat_axis=0)
        return 0.5 * vector + jnp.sum(moved, axis=0)

    length = jnp.sqrt(total(r, r) + EPS)
    basis = [r / column(length)]
    entries = [length]
    for _ in range(2):
        image = apply(basis[-1])
        coeffs = [total(member, image) for member in basis]
        remainder = image
        for member, coeff in zip(basis, coeffs):
            remainder = remainder - column(coeff) * member
        length = jnp.sqrt(total(remainder, remainder) + EPS)
        basis.append(remainder / column(length))
        entries += coeffs + [length]
    return jnp.swapaxes(basis[-1], 0, 1).reshape(OBJ, CL_DEV * LEAF), jnp.stack(entries)


def on_device(r0, near_tiles, nt, ns, nc, far_left, far_right, ft, fs, fc):
    indices = (nt, ns, nc, ft, fs, fc)
    blocks = (near_tiles, jnp.swapaxes(far_left, 1, 2), jnp.swapaxes(far_right, 1, 2))
    r = jnp.swapaxes(r0.reshape(OBJ, CL_DEV, LEAF), 0, 1)

    lists = (nt, ns, ft, fs, nc, fc)
    applied = scatter_sum(*product(lists, gather_targets(r, SCALE_R), blocks, True))
    u = 0.5 * r + applied * (1.0 / SCALE)
    applied = scatter_sum(*product(lists, gather_targets(u, SCALE), blocks, False))
    w = 0.5 * u + applied * (1.0 / SCALE)
    dots = [dot(r, r), dot(r, u), dot(u, u), dot(r, w), dot(u, w), dot(w, w)]
    local = jnp.concatenate(dots + [jnp.zeros((LEAF - len(dots) * OBJ,), jnp.float32)])[None]
    chip = local + lax.ppermute(local, "core", [(0, 1), (1, 0)])
    sums = jnp.sum(to_all(chip, ("gx", "gy", "gq")), axis=0)[0]
    sums = jnp.stack([sums[i * OBJ : (i + 1) * OBJ] for i in range(len(dots))])
    basis_3, entries, fails = pl.pallas_call(
        finish,
        out_shape=(
            jax.ShapeDtypeStruct((OBJ, CL_DEV * LEAF), jnp.float32),
            jax.ShapeDtypeStruct((6, OBJ), jnp.float32),
            jax.ShapeDtypeStruct((1,), jnp.int32),
        ),
        in_specs=[VMEM] * 4,
        out_specs=(VMEM, VMEM, SMEM),
        compiler_params=pltpu.CompilerParams(vmem_limit_bytes=2 * 1024 * 1024),
    )(sums, r0, u, applied)
    def branch():
        plain = plainly(r0, indices, (near_tiles, far_left, far_right))
        return tuple(jnp.where(fails[0] > 0, new, old) for new, old in zip(plain, (basis_3, entries)))

    basis_3, entries = lax.switch(fails[0], (lambda: (basis_3, entries), branch))
    return basis_3, entries.T


def solution(mesh):
    fine = Mesh(mesh.devices.reshape(4, 8, 4, 2), ALL)
    spread = P(ALL)
    return jax.shard_map(
        on_device,
        mesh=fine,
        in_specs=(P(None, ALL),) + (spread,) * 9,
        out_specs=(P(None, ALL), P()),
        check_vma=False,
    )
```
